512 devices in a mesh: seq: 32 (over z_hi, y, core), tensor: 16 (over x, z_lo).
Axes of the slice: x: 4, y: 8, z: 8 (z_hi: 2, z_lo: 4; z = z_hi * 4 + z_lo), core: 2. Of those that a mesh axis runs over, the one named last changes fastest.
Arguments:
- hidden_in: bfloat16 [8192, 5376], P('seq', 'tensor'), may hold values from -128 to 128
- positions: int32 [8192], P('seq'), may hold values from 0 to 16382, as said below
- pre_gain: float32 [5376], replicated, may hold values from -0.5 to 1.5
- query_weight: bfloat16 [5376, 4096], P('seq', 'tensor')
- key_weight: bfloat16 [5376, 2048], P('seq', 'tensor')
- value_weight: bfloat16 [5376, 2048], P('seq', 'tensor'), may hold values from -0.078125 to 0.078125
- query_gain: float32 [128], replicated, may hold values from -0.3 to 4.5
- key_gain: float32 [128], replicated, may hold values from -0.3 to 4.5
- output_weight: bfloat16 [4096, 5376], P('tensor', 'seq')
- post_gain: float32 [5376], P('tensor'), may hold values from -0.5 to 1.5
Outputs:
- hidden_out: bfloat16 [8192, 5376], P('seq', 'tensor')
The draws below stay inside these ranges and needn't reach their ends.
Inputs may be any that keep to these rules, and one draw needn't show every extreme that they name: `positions`: 0 at a prompt's first token, else one more than the position of the token before; the window's first token continues a prompt begun before the window, and some later token starts a new prompt.
All inputs are finite; a program needn't handle non-finite values.
Results may differ from the reference program's by a relative error of at most 0.013.
Values may be sent and summed in bfloat16 or wider, within the bound.
A program may use at most 64 MiB of HBM per device.

```python
import math
import jax
import jax.numpy as jnp
from jax import lax

D = 5376
HEAD_DIM = 128
WINDOW = 1024
KV_HEADS = 16
HEADS = 32
TOKENS = 8192
N_TENSOR = 16


def bounded_normal(key, shape):
    return jax.random.truncated_normal(key, -5.0, 5.0, shape, jnp.float32)


def query_columns(key):
    return bounded_normal(jax.random.fold_in(key, 17), (D, HEADS * HEAD_DIM)) / math.sqrt(D)


def draw_hidden_in(key, part):
    key_core, key_rows, key_cols = jax.random.split(jax.random.fold_in(key, 3), 3)
    row_scale = 10.0 ** jax.random.uniform(key_rows, (TOKENS, 1), jnp.float32)
    col_scale = 10.0 ** jax.random.uniform(key_cols, (1, D), jnp.float32)
    core = bounded_normal(key_core, (TOKENS, D))
    return (core * row_scale * col_scale / 4.0).astype(jnp.bfloat16)


def draw_positions(key, part):
    key_reset, key_forced = jax.random.split(jax.random.fold_in(key, 5), 2)
    index = jnp.arange(TOKENS, dtype=jnp.int32)
    resets = jax.random.randint(key_reset, (TOKENS,), 0, 2 * WINDOW) == 0
    forced = jax.random.randint(key_forced, (), 1, TOKENS)
    resets = (resets | (index == forced)) & (index > 0)
    latest = lax.cummax(jnp.where(resets, index, -1), axis=0)
    first_reset = jnp.min(jnp.where(resets, index, TOKENS))
    begin = 2 * TOKENS - 1 - first_reset
    return jnp.where(latest >= 0, index - latest, index + begin).astype(jnp.int32)


def draw_query_weight(key, part):
    return query_columns(key).astype(jnp.bfloat16)


def draw_key_weight(key, part):
    matrix = bounded_normal(jax.random.fold_in(key, 29), (D, KV_HEADS * HEAD_DIM)) / math.sqrt(D)
    return matrix.astype(jnp.bfloat16)


def gain_values(key):
    return jax.random.uniform(key, (HEAD_DIM,), jnp.float32, -0.3, 0.5)


def draw_query_gain(key, part):
    return gain_values(jax.random.fold_in(key, 41))


def draw_key_gain(key, part):
    return gain_values(jax.random.fold_in(key, 43))


def draw_output_weight(key, part):
    key_base, key_spread = jax.random.split(jax.random.fold_in(key, 53))
    base = bounded_normal(key_base, (HEADS * HEAD_DIM, D))
    ramp = 1.0 + 2.0 * jnp.arange(D, dtype=jnp.float32)[None, :] / D
    spread = 10.0 ** jax.random.uniform(key_spread, (1, D), jnp.float32)
    return (base / math.sqrt(HEADS * HEAD_DIM) * ramp * spread / 3.0).astype(jnp.bfloat16)


def shard_levels(stream_key, shape, shards, least, high):
    level = 1.0
    for axis_at, blocks in shards:
        heights = jax.random.uniform(jax.random.fold_in(jax.random.fold_in(stream_key, 6), axis_at), (blocks,), jnp.float32, least / len(shards), high / len(shards))
        level = level * jnp.repeat(jnp.exp(heights), shape[axis_at] // blocks).reshape((-1,) + (1,) * (len(shape) - 1 - axis_at))
    return level


def centred(rng, extent, width, bound, pieces=(), kind=jnp.bfloat16):
    array = width * jax.random.normal(rng, extent, jnp.float32)
    if pieces:
        array = array * shard_levels(rng, extent, pieces, -0.22, 0.18)
    return jnp.clip(array, -bound, bound).astype(kind)


def setup_inputs(seed: int = 0) -> dict:
    key_list = jax.random.split(jax.random.key(seed), 11)
    hidden_in = draw_hidden_in(jax.random.fold_in(key_list[10], 71), 0)
    positions = draw_positions(jax.random.fold_in(key_list[10], 71), 0)
    pre_gain = jnp.clip(jax.random.uniform(key_list[2], (D,), jnp.float32, -0.5, 1.5), -0.5, 1.5)
    query_weight = draw_query_weight(jax.random.fold_in(key_list[10], 71), 0)
    key_weight = draw_key_weight(jax.random.fold_in(key_list[10], 71), 0)
    value_weight = centred(key_list[5], (D, KV_HEADS * HEAD_DIM), D ** -0.5, 0.078125, ((0, 32), (1, 16)))
    query_gain = draw_query_gain(jax.random.fold_in(key_list[10], 71), 0)
    key_gain = draw_key_gain(jax.random.fold_in(key_list[10], 71), 0)
    output_weight = draw_output_weight(jax.random.fold_in(key_list[10], 71), 0)
    post_gain = jnp.clip(-0.5 + 2.0 * jax.random.uniform(key_list[9], (D,), jnp.float32) ** shard_levels(key_list[9], (D,), ((0, 16),), -0.2, 0.2), -0.5, 1.5)
    return dict(hidden_in=hidden_in, positions=positions, pre_gain=pre_gain, query_weight=query_weight, key_weight=key_weight, value_weight=value_weight, query_gain=query_gain, key_gain=key_gain, output_weight=output_weight, post_gain=post_gain)


epsilon = 1e-06
query_scalar = 168.0
rope_base = 10000.0
masked_score = -1e+30

def rms_scale(values):
    return values * lax.rsqrt(lax.optimization_barrier(jnp.mean(values * values, axis=-1, keepdims=True)) + epsilon)

def rotary(values, token_positions):
    half_dim = values.shape[-1] // 2
    exponent = jnp.arange(half_dim, dtype=jnp.float32) * 2.0 / values.shape[-1]
    inverse = 1.0 / rope_base ** exponent
    angles = token_positions.astype(jnp.float32)[:, None] * inverse[None, :]
    cosine = jnp.cos(angles)[:, None, :]
    sine = jnp.sin(angles)[:, None, :]
    first_half = values[..., :half_dim]
    second_half = values[..., half_dim:]
    return jnp.concatenate([first_half * cosine - second_half * sine, second_half * cosine + first_half * sine], axis=-1)

def reference(hidden_in, positions, pre_gain, query_weight, key_weight, value_weight, query_gain, key_gain, output_weight, post_gain):
    stream = hidden_in.astype(jnp.float32)
    normed = (rms_scale(stream) * (1.0 + pre_gain)).astype(jnp.bfloat16)
    query_raw = jnp.dot(normed, query_weight, preferred_element_type=jnp.float32).reshape(TOKENS, HEADS, HEAD_DIM)
    key_raw = jnp.dot(normed, key_weight, preferred_element_type=jnp.float32).reshape(TOKENS, KV_HEADS, HEAD_DIM)
    value_raw = jnp.dot(normed, value_weight, preferred_element_type=jnp.float32).reshape(TOKENS, KV_HEADS, HEAD_DIM)
    queries = rotary(rms_scale(query_raw) * (1.0 + query_gain), positions).astype(jnp.bfloat16)
    queries = queries.reshape(TOKENS, KV_HEADS, 2, HEAD_DIM)
    keys = rotary(rms_scale(key_raw) * (1.0 + key_gain), positions).astype(jnp.bfloat16)
    values = value_raw.astype(jnp.bfloat16)
    pad_block = jnp.zeros((WINDOW, KV_HEADS, HEAD_DIM), jnp.bfloat16)
    keys_padded = jnp.concatenate([pad_block, keys], axis=0)
    values_padded = jnp.concatenate([pad_block, values], axis=0)

    def attend_block(block_id):
        first = (block_id * WINDOW).astype(jnp.int32)
        query_block = lax.dynamic_slice_in_dim(queries, first, WINDOW, 0).astype(jnp.float32)
        key_block = lax.dynamic_slice_in_dim(keys_padded, first, 2 * WINDOW, 0).astype(jnp.float32)
        value_block = lax.dynamic_slice_in_dim(values_padded, first, 2 * WINDOW, 0).astype(jnp.float32)
        position_block = lax.dynamic_slice_in_dim(positions, first, WINDOW, 0)
        query_index = first + jnp.arange(WINDOW, dtype=jnp.int32)
        key_index = first - WINDOW + jnp.arange(2 * WINDOW, dtype=jnp.int32)
        gap = query_index[:, None] - key_index[None, :]
        allowed = (gap >= 0) & (gap < WINDOW) & (gap <= position_block[:, None]) & (key_index >= 0)[None, :]
        scores = jnp.einsum('qgrd,kgd->grqk', query_block, key_block) * query_scalar ** (-0.5)
        scores = jnp.where(allowed[None, None], scores, masked_score)
        peak = lax.optimization_barrier(jnp.max(scores, axis=-1, keepdims=True))
        expo = jnp.exp(scores - peak)
        weights = (expo / lax.optimization_barrier(jnp.sum(expo, axis=-1, keepdims=True))).astype(jnp.bfloat16)
        context = jnp.einsum('grqk,kgd->qgrd', weights.astype(jnp.float32), value_block)
        return context.astype(jnp.bfloat16).reshape(WINDOW, HEADS * HEAD_DIM)
    blocks = lax.map(attend_block, jnp.arange(TOKENS // WINDOW, dtype=jnp.int32))
    context = blocks.reshape(TOKENS, N_TENSOR, HEADS * HEAD_DIM // N_TENSOR)
    grouped_weight = output_weight.reshape(N_TENSOR, HEADS * HEAD_DIM // N_TENSOR, D)

    def add_group(running, pair):
        context_part, weight_part = pair
        partial_value = jnp.dot(context_part, weight_part, preferred_element_type=jnp.float32)
        rounded = lax.optimization_barrier(partial_value.astype(jnp.bfloat16))
        return (running + rounded.astype(jnp.float32), None)
    attention, unused = lax.scan(add_group, jnp.zeros((TOKENS, D), jnp.float32), (jnp.moveaxis(context, 1, 0), grouped_weight))
    post = rms_scale(attention) * (1.0 + post_gain)
    return (stream + post).astype(jnp.bfloat16)
```

```python
import jax
import jax.numpy as jnp
from jax import lax
from jax.experimental import pallas as pl
from jax.experimental.pallas import tpu as pltpu
from jax.sharding import PartitionSpec as P

D = 5376
HEAD_DIM = 128
WINDOW = 1024
FEAT = 336
HALF = 168
TOK = 256
EPS = 1e-6
SCORE_SCALE = 168.0**-0.5
LOG2E = 1.4426950408889634
MESH = pl.DeviceIdType.MESH
F32 = jnp.float32
BF16 = jnp.bfloat16

REACH = ((4, 3), (3, 4))


def kernel(
    h_ref,
    pos_ref,
    gain_ref,
    wq_ref,
    wk_ref,
    wv_ref,
    qg_ref,
    kg_ref,
    wo_ref,
    pg_ref,
    inv_ref,
    out_ref,
    xg,
    xt,
    wb,
    ws,
    tmp,
    cst,
    kv,
    qb,
    ctx,
    acc,
    sq,
    trig,
    oacc,
    zpart,
    xpart,
    zs,
    zr,
    xs,
    xr,
    rs,
    rr,
    ps,
    pr,
    bs,
    br,
    ms,
    mr,
    hs,
    hr,
    qs,
    qr,
    loc,
):
    s = lax.axis_index("seq")
    t = lax.axis_index("tensor")
    core = lax.rem(s, 2)
    c = s // 2
    y = lax.rem(c, 8)
    zh = c // 8
    x = t // 4
    zl = lax.rem(t, 4)
    other = 1 - core

    def at_seq(chip, which):
        return {"seq": chip * 2 + which, "tensor": t}

    def at_tensor(xx, zz):
        return {"seq": s, "tensor": lax.rem(xx + 8, 4) * 4 + zz}

    sibling = at_seq(c, other)
    far_half = at_seq((1 - zh) * 8 + y, core)
    y_up = at_seq(zh * 8 + lax.rem(y + 1, 8), core)
    y_down = at_seq(zh * 8 + lax.rem(y + 7, 8), core)
    next_chip = at_seq(lax.rem(c + 1, 16), core)
    prev_chip = at_seq(lax.rem(c + 15, 16), core)
    mirror = {"seq": t * 2 + core, "tensor": c}
    off_diagonal = c != t

    pending = []

    def send(src, dst, ssem, rsem, dev, cond=None):
        copy = pltpu.make_async_remote_copy(
            src_ref=src, dst_ref=dst, send_sem=ssem, recv_sem=rsem, device_id=dev, device_id_type=MESH
        )
        if cond is None:
            copy.start()
        else:
            pl.when(cond)(copy.start)
        pending.append((copy, cond))

    def recv(dst, ssem, rsem, cond=None):
        copy = pltpu.make_async_remote_copy(
            src_ref=dst, dst_ref=dst, send_sem=ssem, recv_sem=rsem, device_id=sibling, device_id_type=MESH
        )
        if cond is None:
            copy.wait_recv()
        else:
            pl.when(cond)(copy.wait_recv)

    barrier = pltpu.get_barrier_semaphore()
    peers = [sibling, far_half, y_up, y_down, next_chip, prev_chip]
    peers += [at_tensor(x + d, zl) for d in (1, 2, 3)]
    peers += [at_tensor(x, lax.rem(zl + d, 4)) for d in (1, 2, 3)]
    for peer in peers:
        pl.semaphore_signal(barrier, inc=1, device_id=peer, device_id_type=MESH)

    @pl.when(off_diagonal)
    def _():
        pl.semaphore_signal(barrier, inc=1, device_id=mirror, device_id_type=MESH)

    xg[t] = h_ref[...]
    gain = 1.0 + gain_ref[...]
    ws[0] = (wk_ref[...].astype(F32) * gain).astype(BF16)
    ws[1] = (wv_ref[...].astype(F32) * gain).astype(BF16)
    ws[2] = (wq_ref[:, 0:128].astype(F32) * gain).astype(BF16)
    ws[3] = (wq_ref[:, 128:256].astype(F32) * gain).astype(BF16)
    ws[4] = wo_ref[:, 0:128]
    ws[5] = wo_ref[:, 128:256]

    pl.semaphore_wait(barrier, jnp.where(off_diagonal, len(peers) + 1, len(peers)))

    def near_z(n):
        if n == 0:
            return zl
        if n == 1:
            return zl + 1 - 2 * lax.rem(zl, 2)
        if n == 2:
            return 2 - zl // 2
        return 3 * (1 - zl // 2)

    class TensorFlow:
        def __init__(self, buf, k):
            self.buf = buf
            self.k = k

        def slot(self, dx, n):
            return lax.rem(x + dx + 4, 4) * 4 + near_z(n)

        def to_x(self, n):
            blk = self.buf.at[self.slot(0, n)]
            for i, d in enumerate((1, -1)):
                send(blk, blk, xs.at[self.k, n, i], xr.at[self.k, n, i], at_tensor(x + d, zl))

        def own(self):
            self.to_x(0)
            blk = self.buf.at[self.slot(0, 0)]
            send(blk, blk, zs.at[self.k, 0], zr.at[self.k, zl], at_tensor(x, lax.rem(zl + 1, 4)), zl < 3)
            send(blk, blk, zs.at[self.k, 4], zr.at[self.k, zl], at_tensor(x, lax.rem(zl + 3, 4)), zl > 0)

        def on_z(self, n):
            q = near_z(n)
            blk = self.buf.at[self.slot(0, n)]
            recv(blk, zs.at[self.k, n], zr.at[self.k, q])
            up = q < zl
            ok = jnp.where(up, zl < 3, zl > 0)
            dev = at_tensor(x, jnp.where(up, lax.rem(zl + 1, 4), lax.rem(zl + 3, 4)))
            send(blk, blk, zs.at[self.k, n], zr.at[self.k, q], dev, ok)
            self.to_x(n)

        def on_x(self, n):
            d = 1 - 2 * lax.rem(core + n, 2)
            for i, dx in enumerate((-1, 1)):
                recv(self.buf.at[self.slot(dx, n)], xs.at[self.k, n, i], xr.at[self.k, n, i])
            blk = self.buf.at[self.slot(-d, n)]
            send(blk, blk, xs.at[self.k, n, 2], xr.at[self.k, n, 2], at_tensor(x + d, zl))

        def on_far(self, n):
            recv(self.buf.at[self.slot(2, n)], xs.at[self.k, n, 2], xr.at[self.k, n, 2])

    def w_slot(part, way, d):
        half = zh if part == 0 else 1 - zh
        yy = lax.rem(y + (8 - d if way == 0 else d), 8)
        return half * 8 + yy

    def ring_send(k, part, way, d):
        if d < REACH[part][way]:
            blk = wb.at[2 * k + core, w_slot(part, way, d)]
            i = (part * 2 + way) * 4 + d
            send(blk, blk, rs.at[k, i], rr.at[k, i], y_up if way == 0 else y_down)

    def relay(k, j):
        blk = wb.at[2 * k + core, j]
        send(blk, blk, bs.at[k, j], br.at[k, j], sibling)

    def on_ring(k, part, way, d):
        j = w_slot(part, way, d)
        i = (part * 2 + way) * 4 + d - 1
        recv(wb.at[2 * k + core, j], rs.at[k, i], rr.at[k, i])
        ring_send(k, part, way, d)
        relay(k, j)

    def on_rings(k, part, d):
        for way in (0, 1):
            if d <= REACH[part][way]:
                on_ring(k, part, way, d)

    def own_ring(k):
        own = wb.at[2 * k + core, c]
        send(own, own, ps.at[k, 1], pr.at[k, 1], far_half)
        for way in (0, 1):
            ring_send(k, 0, way, 0)
        relay(k, c)

    def on_half(k):
        j = (1 - zh) * 8 + y
        recv(wb.at[2 * k + core, j], ps.at[k, 1], pr.at[k, 1])
        for way in (0, 1):
            ring_send(k, 1, way, 0)
        relay(k, j)

    def swapped(k):
        recv(tmp.at[k], ps.at[k, 0], pr.at[k, 0])
        mine = ws[2 * k + core].astype(F32)
        theirs = tmp[k].astype(F32)
        low = jnp.where(core == 0, mine, theirs)
        high = jnp.where(core == 0, theirs, mine)
        return jnp.concatenate([low, high], axis=0).astype(BF16)

    hidden = TensorFlow(xg, 0)
    for k in range(3):
        send(ws.at[2 * k + other], tmp.at[k], ps.at[k, 0], pr.at[k, 0], sibling)
    hidden.own()
    for k in range(2):
        wb[2 * k + core, c] = swapped(k)
        own_ring(k)
    cst[...] = swapped(2)

    pos_wide = jnp.transpose(jnp.broadcast_to(pos_ref[...].astype(F32), (HEAD_DIM, TOK)))
    angles = pos_wide * inv_ref[...]
    lane = lax.broadcasted_iota(jnp.int32, (TOK, HEAD_DIM), 1)
    trig[0] = jnp.cos(angles)
    sine = jnp.sin(angles)
    trig[1] = jnp.where(lane < HEAD_DIM // 2, -sine, sine)

    sq[...] = jnp.zeros_like(sq)

    def take(j):
        block = xg[j].astype(F32)
        xt[j] = jnp.transpose(block).astype(BF16)
        sq[0:1, :] += jnp.sum(block * block, axis=0, keepdims=True)

    def on_x(n):
        hidden.on_x(n)
        take(hidden.slot(-1, n))
        take(hidden.slot(1, n))

    def on_z(n):
        hidden.on_z(n)
        take(hidden.slot(0, n))

    def on_far(n):
        hidden.on_far(n)
        take(hidden.slot(2, n))

    take(t)
    on_rings(0, 0, 1)
    on_x(0)
    on_z(1)
    on_rings(1, 0, 1)
    on_rings(0, 0, 2)
    on_half(0)
    on_z(2)
    on_rings(1, 0, 2)
    on_far(0)
    on_half(1)
    on_x(1)
    on_rings(0, 1, 1)
    on_rings(0, 0, 3)
    on_z(3)
    on_rings(1, 0, 3)
    on_rings(0, 1, 2)
    on_far(1)
    on_x(2)
    on_rings(1, 1, 1)
    on_rings(0, 0, 4)
    on_rings(1, 1, 2)
    on_rings(0, 1, 3)
    on_far(2)
    on_x(3)

    send(cst, wb.at[4 + core, t], ms.at[0], mr.at[0], mirror, off_diagonal)

    @pl.when(jnp.logical_not(off_diagonal))
    def _():
        local = pltpu.make_async_copy(cst, wb.at[4 + core, c], loc)
        local.start()
        local.wait()

    on_rings(1, 0, 4)
    on_rings(1, 1, 3)
    on_rings(0, 1, 4)
    on_far(3)

    mean_sq = jnp.transpose(jnp.broadcast_to(sq[0:1, :], (HEAD_DIM, TOK))) / D
    recv(wb.at[4 + core, c], ms.at[0], mr.at[0], off_diagonal)
    own_ring(2)

    def project(k):
        acc[...] = jnp.zeros_like(acc)

        def step(j, carry):
            recv(wb.at[2 * k + other, j], bs.at[k, j], br.at[k, j])
            both = jnp.concatenate([wb[2 * k, j], wb[2 * k + 1, j]], axis=1)
            acc[...] += jnp.dot(xt[j], both, preferred_element_type=F32)
            return carry

        lax.fori_loop(0, 16, step, 0)

    def head(raw, gain_row):
        mean = jnp.mean(raw * raw, axis=-1, keepdims=True)
        unit = raw * lax.rsqrt(mean + EPS * (mean_sq + EPS)) * (1.0 + gain_row)
        return unit * trig[0] + pltpu.roll(unit, HEAD_DIM // 2, 1) * trig[1]

    project(0)
    kv[4, 0] = head(acc[:, 0:128], kg_ref[...]).astype(BF16)
    kv[4, 1] = (acc[:, 128:256] * lax.rsqrt(mean_sq + EPS)).astype(BF16)

    send(kv.at[4], kv.at[2], hs.at[0], hr.at[2], next_chip, c < 15)
    send(kv.at[4], kv.at[3], hs.at[2], hr.at[3], sibling, core == 0)
    for i in range(4):

        @pl.when(s + i < 4)
        def _():
            kv[i] = jnp.zeros((2, TOK, HEAD_DIM), BF16)

    on_rings(1, 1, 4)
    on_half(2)
    on_rings(2, 0, 1)
    project(1)
    recv(kv.at[2], hs.at[0], hr.at[2], c >= 1)
    send(kv.at[2], kv.at[0], hs.at[1], hr.at[0], next_chip, jnp.logical_and(c >= 1, c < 15))
    send(kv.at[2], kv.at[1 + 2 * core], hs.at[3], hr.at[1 + 2 * core], sibling, c >= 1)
    for i in range(2):
        qb[i] = head(acc[:, i * 128 : (i + 1) * 128], qg_ref[...]).astype(BF16)
    on_rings(2, 0, 2)
    on_rings(2, 1, 1)
    recv(kv.at[0], hs.at[1], hr.at[0], c >= 2)
    send(kv.at[0], kv.at[1], hs.at[4], hr.at[1], sibling, jnp.logical_and(c >= 2, core == 1))
    recv(kv.at[3], hs.at[2], hr.at[3], s >= 1)
    on_rings(2, 0, 3)
    on_rings(2, 1, 2)
    recv(kv.at[1], hs.at[3], hr.at[1], s >= 3)

    ROWS = 128

    def attend(step, carry):
        r = lax.rem(step, 2)
        hd = step // 2
        rows = pl.ds(pl.multiple_of(r * ROWS, ROWS), ROWS)
        query = qb[hd, rows, :]
        position = jnp.transpose(jnp.broadcast_to(pos_ref[...], (HEAD_DIM, TOK)).astype(F32)[:, 0:ROWS])
        position = jnp.where(
            r == 0,
            position,
            jnp.transpose(jnp.broadcast_to(pos_ref[...], (HEAD_DIM, TOK)).astype(F32)[:, ROWS:TOK]),
        ).astype(jnp.int32)
        position = jnp.concatenate([position, position], axis=1)
        row = lax.broadcasted_iota(jnp.int32, (ROWS, TOK), 0) + r * ROWS
        col = lax.broadcasted_iota(jnp.int32, (ROWS, TOK), 1)
        limit = jnp.minimum(jnp.minimum(position, row + s * TOK), WINDOW - 1)
        scores = []
        for i in range(5):
            raw = lax.dot_general(query, kv[i, 0], (((1,), (1,)), ((), ())), preferred_element_type=F32)
            gap = row + (4 - i) * TOK - col
            allowed = gap <= limit
            if i == 4:
                allowed = jnp.logical_and(allowed, gap >= 0)
            scores.append(jnp.where(allowed, raw, -1e30))
        peak = scores[0]
        for i in range(1, 5):
            peak = jnp.maximum(peak, scores[i])
        peak = jnp.max(peak, axis=-1, keepdims=True)
        total = jnp.zeros((ROWS, TOK), F32)
        mixed = jnp.zeros((ROWS, HEAD_DIM), F32)
        for i in range(5):
            expo = jnp.exp2((scores[i] - peak) * (SCORE_SCALE * LOG2E))
            total += expo
            mixed += jnp.dot(expo.astype(BF16), kv[i, 1], preferred_element_type=F32)
        mixed = mixed / jnp.sum(total, axis=-1, keepdims=True)
        ctx[t, hd, rows, :] = mixed.astype(BF16)
        return carry

    lax.fori_loop(0, 4, attend, 0)

    context = TensorFlow(ctx, 1)
    context.own()
    on_rings(2, 0, 4)
    on_rings(2, 1, 3)
    on_rings(2, 1, 4)

    def wait_out(j, carry):
        recv(wb.at[4 + other, j], bs.at[2, j], br.at[2, j])
        return carry

    lax.fori_loop(0, 16, wait_out, 0)
    oacc[...] = jnp.zeros_like(oacc)

    def out_step(j):
        left = jnp.concatenate([wb[4, j], wb[5, j]], axis=1)
        right = jnp.concatenate([ctx[j, 0], ctx[j, 1]], axis=1)
        oacc[...] += lax.dot_general(left, right, (((1,), (1,)), ((), ())), preferred_element_type=F32)

    def c_x(n):
        context.on_x(n)
        out_step(context.slot(-1, n))
        out_step(context.slot(1, n))

    def c_z(n):
        context.on_z(n)
        out_step(context.slot(0, n))

    def c_far(n):
        context.on_far(n)
        out_step(context.slot(2, n))

    out_step(t)
    c_z(1)
    c_x(0)
    c_z(2)
    c_x(1)
    c_far(0)
    c_z(3)
    c_x(2)
    c_far(1)
    c_x(3)
    c_far(2)
    c_far(3)

    def spread(buf, k, me, device):
        for i, d in enumerate((1, 2, 3)):
            send(buf.at[me], buf.at[me], qs.at[k, i], qr.at[k, me], device(lax.rem(me + d, 4)))
        for d in (1, 2, 3):
            j = lax.rem(me + d, 4)
            recv(buf.at[j], qs.at[k, d - 1], qr.at[k, j])
        return buf[0] + buf[1] + buf[2] + buf[3]

    attention = oacc[...]
    zpart[zl] = jnp.broadcast_to(jnp.sum(attention * attention, axis=0, keepdims=True), (8, TOK))
    xpart[x] = spread(zpart, 0, zl, lambda j: at_tensor(x, j))
    squares = spread(xpart, 1, x, lambda j: at_tensor(j, zl))
    scale = lax.rsqrt(squares[0:1, :] / D + EPS)
    post = oacc[...] * scale * (1.0 + pg_ref[...])
    out_ref[...] = (h_ref[...].astype(F32) + post).astype(BF16)

    for copy, cond in pending:
        if cond is None:
            copy.wait_send()
        else:
            pl.when(cond)(copy.wait_send)


def body(
    hidden_in,
    positions,
    pre_gain,
    query_weight,
    key_weight,
    value_weight,
    query_gain,
    key_gain,
    output_weight,
    post_gain,
):
    s = lax.axis_index("seq")
    exponent = jnp.arange(HEAD_DIM // 2, dtype=F32) * 2.0 / HEAD_DIM
    inverse = 1.0 / 10000.0**exponent
    inverse = jnp.concatenate([inverse, inverse])[None, :]
    gain = lax.dynamic_slice(pre_gain, (s * HALF,), (HALF,)).reshape(HALF, 1)
    vmem = pl.BlockSpec(memory_space=pltpu.VMEM)
    dma = pltpu.SemaphoreType.DMA
    out = pl.pallas_call(
        kernel,
        out_shape=jax.ShapeDtypeStruct((FEAT, TOK), BF16),
        in_specs=[vmem] * 11,
        out_specs=vmem,
        scratch_shapes=[
            pltpu.VMEM((16, FEAT, TOK), BF16),
            pltpu.VMEM((16, TOK, FEAT), BF16),
            pltpu.VMEM((6, 16, FEAT, 128), BF16),
            pltpu.VMEM((6, HALF, 128), BF16),
            pltpu.VMEM((3, HALF, 128), BF16),
            pltpu.VMEM((FEAT, 128), BF16),
            pltpu.VMEM((5, 2, TOK, HEAD_DIM), BF16),
            pltpu.VMEM((2, TOK, HEAD_DIM), BF16),
            pltpu.VMEM((16, 2, TOK, HEAD_DIM), BF16),
            pltpu.VMEM((TOK, 256), F32),
            pltpu.VMEM((8, TOK), F32),
            pltpu.VMEM((2, TOK, HEAD_DIM), F32),
            pltpu.VMEM((FEAT, TOK), F32),
            pltpu.VMEM((4, 8, TOK), F32),
            pltpu.VMEM((4, 8, TOK), F32),
            dma((2, 5)),
            dma((2, 4)),
            dma((2, 4, 3)),
            dma((2, 4, 3)),
            dma((3, 16)),
            dma((3, 16)),
            dma((3, 2)),
            dma((3, 2)),
            dma((3, 16)),
            dma((3, 16)),
            dma((1,)),
            dma((1,)),
            dma((5,)),
            dma((5,)),
            dma((2, 3)),
            dma((2, 4)),
            dma,
        ],
        compiler_params=pltpu.CompilerParams(
            collective_id=0, has_side_effects=True, vmem_limit_bytes=56 << 20
        ),
        cost_estimate=pl.CostEstimate(flops=3_000_000_000, bytes_accessed=1_000_000, transcendentals=1_000_000),
    )(
        hidden_in.T,
        positions[None, :],
        gain,
        query_weight,
        key_weight,
        value_weight,
        query_gain[None, :],
        key_gain[None, :],
        output_weight.T,
        post_gain[:, None],
        inverse,
    )
    return out.T


def solution(mesh):
    placed = (
        P("seq", "tensor"),
        P("seq"),
        P(),
        P("seq", "tensor"),
        P("seq", "tensor"),
        P("seq", "tensor"),
        P(),
        P(),
        P("tensor", "seq"),
        P("tensor"),
    )
    return jax.shard_map(
        body, mesh=mesh, in_specs=placed, out_specs=P("seq", "tensor"), check_vma=False
    )
```

```python
import jax
import jax.numpy as jnp
import numpy as np
from jax import lax
from jax.experimental import pallas as pl
from jax.experimental.pallas import tpu as pltpu
from jax.sharding import PartitionSpec as P

D = 5376
HEAD_DIM = 128
WINDOW = 1024
FEAT = 336
HALF = 168
TOK = 256
EPS = 1e-6
SCORE_SCALE = 168.0**-0.5
LOG2E = 1.4426950408889634
MESH = pl.DeviceIdType.MESH
F32 = jnp.float32
BF16 = jnp.bfloat16

REACH = ((4, 3), (3, 4))
KV, Q, OUT = 0, 1, 2
NT = (((1,), (1,)), ((), ()))


def kernel(
    h_ref,
    pos_ref,
    gain_ref,
    wq_ref,
    wk_ref,
    wv_ref,
    qg_ref,
    kg_ref,
    wo_ref,
    pg_ref,
    inv_ref,
    out_ref,
    xg,
    xt,
    wb,
    kv,
    qb,
    ctx,
    acc,
    sq,
    trig,
    oacc,
    zpart,
    xpart,
    zs,
    zr,
    xs,
    xr,
    rs,
    rr,
    ps,
    pr,
    bs,
    br,
    ms,
    mr,
    hs,
    hr,
    qs,
    qr,
    loc,
):
    s = lax.axis_index("seq")
    t = lax.axis_index("tensor")
    core = lax.rem(s, 2)
    c = s // 2
    y = lax.rem(c, 8)
    zh = c // 8
    x = t // 4
    zl = lax.rem(t, 4)
    other = 1 - core

    def at_seq(chip, which):
        return {"seq": chip * 2 + which, "tensor": t}

    def at_tensor(xx, zz):
        return {"seq": s, "tensor": lax.rem(xx + 8, 4) * 4 + zz}

    sibling = at_seq(c, other)
    far_half = at_seq((1 - zh) * 8 + y, core)
    y_up = at_seq(zh * 8 + lax.rem(y + 1, 8), core)
    y_down = at_seq(zh * 8 + lax.rem(y + 7, 8), core)
    next_chip = at_seq(lax.rem(c + 1, 16), core)
    prev_chip = at_seq(lax.rem(c + 15, 16), core)
    mirror = {"seq": t * 2 + core, "tensor": c}
    off_diagonal = c != t

    pending = []

    def send(src, dst, ssem, rsem, dev, cond=None):
        copy = pltpu.make_async_remote_copy(
            src_ref=src, dst_ref=dst, send_sem=ssem, recv_sem=rsem, device_id=dev, device_id_type=MESH
        )
        if cond is None:
            copy.start()
        else:
            pl.when(cond)(copy.start)
        pending.append((copy, cond))

    def recv(dst, ssem, rsem, cond=None):
        copy = pltpu.make_async_remote_copy(
            src_ref=dst, dst_ref=dst, send_sem=ssem, recv_sem=rsem, device_id=sibling, device_id_type=MESH
        )
        if cond is None:
            copy.wait_recv()
        else:
            pl.when(cond)(copy.wait_recv)

    barrier = pltpu.get_barrier_semaphore()
    peers = [sibling, far_half, y_up, y_down, next_chip, prev_chip]
    peers += [at_tensor(x + d, zl) for d in (1, 2, 3)]
    peers += [at_tensor(x, lax.rem(zl + d, 4)) for d in (1, 2, 3)]
    for peer in peers:
        pl.semaphore_signal(barrier, inc=1, device_id=peer, device_id_type=MESH)

    @pl.when(off_diagonal)
    def _():
        pl.semaphore_signal(barrier, inc=1, device_id=mirror, device_id_type=MESH)

    xg[t] = h_ref[...]
    first = s * HALF
    row0 = first // 128
    index = lax.broadcasted_iota(jnp.int32, (HALF, 128), 0) + (first - row0 * 128)
    lanes = lax.broadcasted_iota(jnp.int32, (HALF, 128), 1)
    gain = jnp.zeros((HALF, 128), F32)
    for i in range(3):
        line = gain_ref[pl.ds(jnp.minimum(row0 + i, D // 128 - 1), 1), :]
        gain = jnp.where(lanes + i * 128 == index, line, gain)
    gain = 1.0 + jnp.sum(gain, axis=1, keepdims=True)
    wb[KV, core, c, :, 0:128] = (wk_ref[...].astype(F32) * gain).astype(BF16)
    wb[KV, core, c, :, 128:256] = (wv_ref[...].astype(F32) * gain).astype(BF16)
    wb[Q, core, c] = (wq_ref[...].astype(F32) * gain).astype(BF16)

    pl.semaphore_wait(barrier, jnp.where(off_diagonal, len(peers) + 1, len(peers)))

    def near_z(n):
        if n == 0:
            return zl
        if n == 1:
            return zl + 1 - 2 * lax.rem(zl, 2)
        if n == 2:
            return 2 - zl // 2
        return 3 * (1 - zl // 2)

    class TensorFlow:
        def __init__(self, k, block):
            self.block = block
            self.k = k

        def slot(self, dx, n):
            return lax.rem(x + dx + 4, 4) * 4 + near_z(n)

        def to_x(self, n):
            blk = self.block(self.slot(0, n))
            for i, d in enumerate((1, 3, 2)):
                send(blk, blk, xs.at[self.k, n, i], xr.at[self.k, n, i], at_tensor(x + d, zl))

        def own(self):
            blk = self.block(t)
            send(blk, blk, zs.at[self.k, 0], zr.at[self.k, zl], at_tensor(x, lax.rem(zl + 1, 4)), zl < 3)
            send(blk, blk, zs.at[self.k, 4], zr.at[self.k, zl], at_tensor(x, lax.rem(zl + 3, 4)), zl > 0)
            self.to_x(0)

        def on_z(self, n):
            q = near_z(n)
            blk = self.block(self.slot(0, n))
            recv(blk, zs.at[self.k, n], zr.at[self.k, q])
            up = q < zl
            ok = jnp.where(up, zl < 3, zl > 0)
            dev = at_tensor(x, jnp.where(up, lax.rem(zl + 1, 4), lax.rem(zl + 3, 4)))
            send(blk, blk, zs.at[self.k, n], zr.at[self.k, q], dev, ok)
            self.to_x(n)

        def on_x(self, n, i):
            d = (1, 3, 2)[i]
            recv(self.block(self.slot(-d, n)), xs.at[self.k, n, i], xr.at[self.k, n, i])

    def w_slot(part, way, d):
        half = zh if part == 0 else 1 - zh
        yy = lax.rem(y + (8 - d if way == 0 else d), 8)
        return half * 8 + yy

    def ring_send(k, part, way, d):
        if d < REACH[part][way]:
            blk = wb.at[k, core, w_slot(part, way, d)]
            i = (part * 2 + way) * 4 + d
            send(blk, blk, rs.at[k, i], rr.at[k, i], y_up if way == 0 else y_down)

    def relay(k, j):
        blk = wb.at[k, core, j]
        send(blk, blk, bs.at[k, j], br.at[k, j], sibling)

    def on_rings(k, part, d):
        for way in (0, 1):
            if d <= REACH[part][way]:
                j = w_slot(part, way, d)
                i = (part * 2 + way) * 4 + d - 1
                recv(wb.at[k, core, j], rs.at[k, i], rr.at[k, i])
                ring_send(k, part, way, d)
                relay(k, j)

    def to_half(k):
        own = wb.at[k, core, c]
        send(own, own, ps.at[k], pr.at[k], far_half)

    def own_ring(k):
        for way in (0, 1):
            ring_send(k, 0, way, 0)

    def on_half(k):
        j = (1 - zh) * 8 + y
        recv(wb.at[k, core, j], ps.at[k], pr.at[k])
        for way in (0, 1):
            ring_send(k, 1, way, 0)
        relay(k, j)

    hidden = TensorFlow(0, lambda j: xg.at[j])
    own_ring(KV)
    to_half(KV)
    hidden.own()
    own_ring(Q)
    to_half(Q)
    relay(KV, c)
    relay(Q, c)

    pos_wide = jnp.transpose(jnp.broadcast_to(pos_ref[...].astype(F32), (HEAD_DIM, TOK)))
    angles = pos_wide * inv_ref[...]
    lane = lax.broadcasted_iota(jnp.int32, (TOK, HEAD_DIM), 1)
    trig[0] = jnp.cos(angles)
    sine = jnp.sin(angles)
    trig[1] = jnp.where(lane < HEAD_DIM // 2, -sine, sine)
    trig[2] = pos_wide

    sq[...] = jnp.zeros_like(sq)

    def take(j):
        block = xg[j].astype(F32)
        xt[j, 0] = jnp.transpose(block[0:HALF]).astype(BF16)
        xt[j, 1] = jnp.transpose(block[HALF:FEAT]).astype(BF16)
        sq[0:1, :] += jnp.sum(block * block, axis=0, keepdims=True)

    def take_x(n, i):
        hidden.on_x(n, i)
        take(hidden.slot(-(1, 3, 2)[i], n))

    def take_z(n):
        take(hidden.slot(0, n))

    on_rings(KV, 0, 1)
    hidden.on_z(1)
    on_rings(Q, 0, 1)
    on_half(KV)
    take(t)
    on_rings(KV, 0, 2)
    take_x(0, 0)
    take_x(0, 1)
    hidden.on_z(2)
    on_half(Q)
    on_rings(Q, 0, 2)
    on_rings(KV, 1, 1)

    send(wo_ref, wb.at[OUT, core, t], ms.at[0], mr.at[0], mirror, off_diagonal)

    @pl.when(jnp.logical_not(off_diagonal))
    def _():
        local = pltpu.make_async_copy(wo_ref, wb.at[OUT, core, c], loc)
        local.start()
        local.wait()

    take_z(1)
    on_rings(KV, 0, 3)
    take_x(0, 2)
    on_rings(Q, 1, 1)
    hidden.on_z(3)
    take_z(2)
    on_rings(Q, 0, 3)
    on_rings(KV, 1, 2)
    take_x(1, 0)
    take_x(1, 1)
    on_rings(KV, 0, 4)
    on_rings(Q, 1, 2)
    take_x(1, 2)
    on_rings(KV, 1, 3)
    on_rings(Q, 0, 4)
    take_x(2, 0)
    take_x(2, 1)
    on_rings(Q, 1, 3)
    on_rings(KV, 1, 4)
    recv(wb.at[OUT, core, c], ms.at[0], mr.at[0], off_diagonal)
    to_half(OUT)
    own_ring(OUT)
    relay(OUT, c)
    take_z(3)
    take_x(2, 2)
    on_rings(Q, 1, 4)
    take_x(3, 0)
    take_x(3, 1)
    take_x(3, 2)

    mean_sq = jnp.transpose(jnp.broadcast_to(sq[0:1, :], (HEAD_DIM, TOK))) / D

    def project(k):
        acc[...] = jnp.zeros_like(acc)

        def step(j, carry):
            recv(wb.at[k, other, j], bs.at[k, j], br.at[k, j])
            acc[...] += jnp.dot(xt[j, 0], wb[k, 0, j], preferred_element_type=F32) + jnp.dot(
                xt[j, 1], wb[k, 1, j], preferred_element_type=F32
            )
            return carry

        lax.fori_loop(0, 16, step, 0)

    def head(raw, gain_row):
        mean = jnp.mean(raw * raw, axis=-1, keepdims=True)
        unit = raw * lax.rsqrt(mean + EPS * (mean_sq + EPS)) * (1.0 + gain_row)
        return unit * trig[0] + pltpu.roll(unit, HEAD_DIM // 2, 1) * trig[1]

    project(KV)
    kv[4, 0] = head(acc[:, 0:128], kg_ref[...]).astype(BF16)
    kv[4, 1] = (acc[:, 128:256] * lax.rsqrt(mean_sq + EPS)).astype(BF16)

    send(kv.at[4], kv.at[2], hs.at[0], hr.at[2], next_chip, c < 15)
    send(kv.at[4], kv.at[3], hs.at[2], hr.at[3], sibling, core == 0)
    for i in range(4):

        @pl.when(s + i < 4)
        def _():
            kv[i] = jnp.zeros((2, TOK, HEAD_DIM), BF16)

    on_half(OUT)
    on_rings(OUT, 0, 1)
    project(Q)
    recv(kv.at[2], hs.at[0], hr.at[2], c >= 1)
    send(kv.at[2], kv.at[0], hs.at[1], hr.at[0], next_chip, jnp.logical_and(c >= 1, c < 15))
    send(kv.at[2], kv.at[1 + 2 * core], hs.at[3], hr.at[1 + 2 * core], sibling, c >= 1)
    for i in range(2):
        qb[i] = head(acc[:, i * 128 : (i + 1) * 128], qg_ref[...]).astype(BF16)
    on_rings(OUT, 0, 2)
    on_rings(OUT, 1, 1)
    recv(kv.at[0], hs.at[1], hr.at[0], c >= 2)
    send(kv.at[0], kv.at[1], hs.at[4], hr.at[1], sibling, jnp.logical_and(c >= 2, core == 1))
    recv(kv.at[3], hs.at[2], hr.at[3], s >= 1)
    on_rings(OUT, 0, 3)
    recv(kv.at[1], hs.at[3], hr.at[1], s >= 3)

    ROWS = 128

    def attend(hd, r):
        rows = pl.ds(pl.multiple_of(r * ROWS, ROWS), ROWS)
        query = qb[hd, rows, :]
        position = trig[2, rows, :].astype(jnp.int32)
        position = jnp.concatenate([position, position], axis=1)
        row = lax.broadcasted_iota(jnp.int32, (ROWS, TOK), 0) + r * ROWS
        col = lax.broadcasted_iota(jnp.int32, (ROWS, TOK), 1)
        limit = jnp.minimum(jnp.minimum(position, row + s * TOK), WINDOW - 1)
        scores = []
        for i in range(5):
            raw = lax.dot_general(query, kv[i, 0], NT, preferred_element_type=F32)
            gap = row + (4 - i) * TOK - col
            allowed = gap <= limit
            if i == 4:
                allowed = jnp.logical_and(allowed, gap >= 0)
            scores.append(jnp.where(allowed, raw, -1e30))
        peak = scores[0]
        for i in range(1, 5):
            peak = jnp.maximum(peak, scores[i])
        peak = jnp.max(peak, axis=-1, keepdims=True)
        total = jnp.zeros((ROWS, TOK), F32)
        mixed = jnp.zeros((ROWS, HEAD_DIM), F32)
        for i in range(5):
            expo = jnp.exp2((scores[i] - peak) * (SCORE_SCALE * LOG2E))
            total += expo
            mixed += jnp.dot(expo.astype(BF16), kv[i, 1], preferred_element_type=F32)
        mixed = mixed / jnp.sum(total, axis=-1, keepdims=True)
        ctx[hd, t, rows, :] = mixed.astype(BF16)

    contexts = []
    for hd in range(2):

        def rows_of(r, carry, hd=hd):
            attend(hd, r)
            return carry

        lax.fori_loop(0, 2, rows_of, 0)
        flow = TensorFlow(1 + hd, lambda j, hd=hd: ctx.at[hd, j])
        flow.own()
        contexts.append(flow)

    on_rings(OUT, 1, 2)
    on_rings(OUT, 0, 4)
    oacc[...] = jnp.zeros_like(oacc)

    def out_step(j):
        right = jnp.concatenate([ctx[0, j], ctx[1, j]], axis=1)
        for i in range(2):
            oacc[i] += lax.dot_general(wb[OUT, i, j], right, NT, preferred_element_type=F32)

    def c_z(n):
        for flow in contexts:
            flow.on_z(n)

    def c_x(n, i):
        for flow in contexts:
            flow.on_x(n, i)
        out_step(contexts[0].slot(-(1, 3, 2)[i], n))

    def out_z(n):
        out_step(contexts[0].slot(0, n))

    c_z(1)
    on_rings(OUT, 1, 3)
    c_z(2)
    on_rings(OUT, 1, 4)
    c_z(3)

    def wait_out(j, carry):
        recv(wb.at[OUT, other, j], bs.at[OUT, j], br.at[OUT, j])
        return carry

    lax.fori_loop(0, 16, wait_out, 0)
    out_step(t)
    for n in range(1, 4):
        out_z(n)
    for n in range(4):
        for i in range(3):
            c_x(n, i)

    def spread(buf, k, me, device):
        for i, d in enumerate((1, 2, 3)):
            send(buf.at[me], buf.at[me], qs.at[k, i], qr.at[k, me], device(lax.rem(me + d, 4)))
        for d in (1, 2, 3):
            j = lax.rem(me + d, 4)
            recv(buf.at[j], qs.at[k, d - 1], qr.at[k, j])
        return buf[0] + buf[1] + buf[2] + buf[3]

    squares = jnp.sum(oacc[0] * oacc[0] + oacc[1] * oacc[1], axis=0, keepdims=True)
    zpart[zl] = jnp.broadcast_to(squares, (8, TOK))
    xpart[x] = spread(zpart, 0, zl, lambda j: at_tensor(x, j))
    squares = spread(xpart, 1, x, lambda j: at_tensor(j, zl))
    scale = lax.rsqrt(squares[0:1, :] / D + EPS)
    diagonal = lax.broadcasted_iota(jnp.int32, (FEAT, FEAT), 0) == lax.broadcasted_iota(
        jnp.int32, (FEAT, FEAT), 1
    )
    post_gain = 1.0 + jnp.sum(jnp.where(diagonal, pg_ref[...][None, :], 0.0), axis=1, keepdims=True)
    attention = jnp.concatenate([oacc[0], oacc[1]], axis=0)
    out_ref[...] = (h_ref[...].astype(F32) + attention * scale * post_gain).astype(BF16)

    for copy, cond in pending:
        if cond is None:
            copy.wait_send()
        else:
            pl.when(cond)(copy.wait_send)


def body(
    hidden_in,
    positions,
    pre_gain,
    query_weight,
    key_weight,
    value_weight,
    query_gain,
    key_gain,
    output_weight,
    post_gain,
):
    exponent = np.arange(HEAD_DIM // 2, dtype=np.float32) * np.float32(2.0) / np.float32(HEAD_DIM)
    inverse = np.float32(1.0) / np.float32(10000.0) ** exponent
    inverse = np.concatenate([inverse, inverse])[None, :].astype(np.float32)
    vmem = pl.BlockSpec(memory_space=pltpu.VMEM)
    dma = pltpu.SemaphoreType.DMA
    out = pl.pallas_call(
        kernel,
        out_shape=jax.ShapeDtypeStruct((FEAT, TOK), BF16),
        in_specs=[vmem] * 11,
        out_specs=vmem,
        scratch_shapes=[
            pltpu.VMEM((16, FEAT, TOK), BF16),
            pltpu.VMEM((16, 2, TOK, HALF), BF16),
            pltpu.VMEM((3, 2, 16, HALF, 256), BF16),
            pltpu.VMEM((5, 2, TOK, HEAD_DIM), BF16),
            pltpu.VMEM((2, TOK, HEAD_DIM), BF16),
            pltpu.VMEM((2, 16, TOK, HEAD_DIM), BF16),
            pltpu.VMEM((TOK, 256), F32),
            pltpu.VMEM((8, TOK), F32),
            pltpu.VMEM((3, TOK, HEAD_DIM), F32),
            pltpu.VMEM((2, HALF, TOK), F32),
            pltpu.VMEM((4, 8, TOK), F32),
            pltpu.VMEM((4, 8, TOK), F32),
            dma((3, 5)),
            dma((3, 4)),
            dma((3, 4, 3)),
            dma((3, 4, 3)),
            dma((3, 16)),
            dma((3, 16)),
            dma((3,)),
            dma((3,)),
            dma((3, 16)),
            dma((3, 16)),
            dma((1,)),
            dma((1,)),
            dma((5,)),
            dma((5,)),
            dma((2, 3)),
            dma((2, 4)),
            dma,
        ],
        compiler_params=pltpu.CompilerParams(
            collective_id=0, has_side_effects=True, vmem_limit_bytes=56 << 20
        ),
        cost_estimate=pl.CostEstimate(flops=3_000_000_000, bytes_accessed=1_000_000, transcendentals=1_000_000),
    )(
        hidden_in.T,
        positions[None, :],
        pre_gain.reshape(D // 128, 128),
        query_weight,
        key_weight,
        value_weight,
        query_gain[None, :],
        key_gain[None, :],
        output_weight.T,
        post_gain,
        inverse,
    )
    return out.T


def solution(mesh):
    placed = (
        P("seq", "tensor"),
        P("seq"),
        P(),
        P("seq", "tensor"),
        P("seq", "tensor"),
        P("seq", "tensor"),
        P(),
        P(),
        P("tensor", "seq"),
        P("tensor"),
    )
    return jax.shard_map(
        body, mesh=mesh, in_specs=placed, out_specs=P("seq", "tensor"), check_vma=False
    )
```

```python
import jax
import jax.numpy as jnp
import numpy as np
from jax import lax
from jax.experimental import pallas as pl
from jax.experimental.pallas import tpu as pltpu
from jax.sharding import PartitionSpec as P

D = 5376
HEAD_DIM = 128
WINDOW = 1024
FEAT = 336
HALF = 168
TOK = 256
EPS = 1e-6
SCORE_SCALE = 168.0**-0.5
LOG2E = 1.4426950408889634
MESH = pl.DeviceIdType.MESH
F32 = jnp.float32
BF16 = jnp.bfloat16

REACH = ((4, 3), (3, 4))
KV, Q, OUT = 0, 1, 2
NT = (((1,), (1,)), ((), ()))


def kernel(
    h_ref,
    pos_ref,
    gain_ref,
    wq_ref,
    wk_ref,
    wv_ref,
    qg_ref,
    kg_ref,
    wo_ref,
    pg_ref,
    inv_ref,
    out_ref,
    xg,
    xt,
    wb,
    kv,
    qb,
    ctx,
    acc,
    sq,
    trig,
    oacc,
    zpart,
    xpart,
    zs,
    zr,
    xs,
    xr,
    rs,
    rr,
    ps,
    pr,
    bs,
    br,
    ms,
    mr,
    hs,
    hr,
    qs,
    qr,
    loc,
):
    s = lax.axis_index("seq")
    t = lax.axis_index("tensor")
    core = lax.rem(s, 2)
    c = s // 2
    y = lax.rem(c, 8)
    zh = c // 8
    x = t // 4
    zl = lax.rem(t, 4)
    other = 1 - core

    def at_seq(chip, which):
        return {"seq": chip * 2 + which, "tensor": t}

    def at_tensor(xx, zz):
        return {"seq": s, "tensor": lax.rem(xx + 8, 4) * 4 + zz}

    sibling = at_seq(c, other)
    far_half = at_seq((1 - zh) * 8 + y, core)
    y_up = at_seq(zh * 8 + lax.rem(y + 1, 8), core)
    y_down = at_seq(zh * 8 + lax.rem(y + 7, 8), core)
    next_chip = at_seq(lax.rem(c + 1, 16), core)
    prev_chip = at_seq(lax.rem(c + 15, 16), core)
    out_home = lax.rem(t, 2) * 8 + lax.rem(y + t // 2, 8)
    out_to = {"seq": out_home * 2 + core, "tensor": c}
    out_from = {"seq": t * 2 + core, "tensor": lax.rem(y + 8 - lax.rem(t, 8), 8) * 2 + zh}
    moves = jnp.logical_or(c != t, out_home != c)

    pending = []

    def send(src, dst, ssem, rsem, dev, cond=None):
        copy = pltpu.make_async_remote_copy(
            src_ref=src, dst_ref=dst, send_sem=ssem, recv_sem=rsem, device_id=dev, device_id_type=MESH
        )
        if cond is None:
            copy.start()
        else:
            pl.when(cond)(copy.start)
        pending.append((copy, cond))

    def recv(dst, ssem, rsem, cond=None):
        copy = pltpu.make_async_remote_copy(
            src_ref=dst, dst_ref=dst, send_sem=ssem, recv_sem=rsem, device_id=sibling, device_id_type=MESH
        )
        if cond is None:
            copy.wait_recv()
        else:
            pl.when(cond)(copy.wait_recv)

    barrier = pltpu.get_barrier_semaphore()
    peers = [sibling, far_half, y_up, y_down, next_chip, prev_chip]
    peers += [at_tensor(x + d, zl) for d in (1, 2, 3)]
    peers += [at_tensor(x, lax.rem(zl + d, 4)) for d in (1, 2, 3)]
    for peer in peers:
        pl.semaphore_signal(barrier, inc=1, device_id=peer, device_id_type=MESH)

    @pl.when(moves)
    def _():
        for peer in (out_to, out_from):
            pl.semaphore_signal(barrier, inc=1, device_id=peer, device_id_type=MESH)

    xg[0, t] = h_ref[:, 0:128]
    xg[1, t] = h_ref[:, 128:256]
    first = s * HALF
    row0 = first // 128
    index = lax.broadcasted_iota(jnp.int32, (HALF, 128), 0) + (first - row0 * 128)
    lanes = lax.broadcasted_iota(jnp.int32, (HALF, 128), 1)
    gain = jnp.zeros((HALF, 128), F32)
    for i in range(3):
        line = gain_ref[pl.ds(jnp.minimum(row0 + i, D // 128 - 1), 1), :]
        gain = jnp.where(lanes + i * 128 == index, line, gain)
    gain = 1.0 + jnp.sum(gain, axis=1, keepdims=True)
    wb[KV, core, c, :, 0:128] = (wk_ref[...].astype(F32) * gain).astype(BF16)
    wb[KV, core, c, :, 128:256] = (wv_ref[...].astype(F32) * gain).astype(BF16)
    wb[Q, core, c] = (wq_ref[...].astype(F32) * gain).astype(BF16)

    pl.semaphore_wait(barrier, jnp.where(moves, len(peers) + 2, len(peers)))

    def near_z(n):
        if n == 0:
            return zl
        if n == 1:
            return zl + 1 - 2 * lax.rem(zl, 2)
        if n == 2:
            return 2 - zl // 2
        return 3 * (1 - zl // 2)

    class TensorFlow:
        def __init__(self, k, block):
            self.block = block
            self.k = k

        def slot(self, dx, n):
            return lax.rem(x + dx + 4, 4) * 4 + near_z(n)

        def way(self, n):
            return lax.rem(core + n, 2)

        def to_x(self, n):
            blk = self.block(self.slot(0, n))
            for i, d in enumerate((1, 3)):
                send(blk, blk, xs.at[self.k, n, i], xr.at[self.k, n, i], at_tensor(x + d, zl))

        def own_z(self):
            blk = self.block(t)
            send(blk, blk, zs.at[self.k, 0], zr.at[self.k, zl], at_tensor(x, lax.rem(zl + 1, 4)), zl < 3)
            send(blk, blk, zs.at[self.k, 4], zr.at[self.k, zl], at_tensor(x, lax.rem(zl + 3, 4)), zl > 0)

        def on_z(self, n):
            q = near_z(n)
            blk = self.block(self.slot(0, n))
            recv(blk, zs.at[self.k, n], zr.at[self.k, q])
            up = q < zl
            ok = jnp.where(up, zl < 3, zl > 0)
            dev = at_tensor(x, jnp.where(up, lax.rem(zl + 1, 4), lax.rem(zl + 3, 4)))
            send(blk, blk, zs.at[self.k, n], zr.at[self.k, q], dev, ok)
            self.to_x(n)

        def relay_x(self, n):
            i = self.way(n)
            d = 1 - 2 * i
            j = self.slot(-d, n)
            recv(self.block(j), xs.at[self.k, n, 0], xr.at[self.k, n, i])
            send(self.block(j), self.block(j), xs.at[self.k, n, 2], xr.at[self.k, n, 2], at_tensor(x + d, zl))
            return j

        def near(self, n):
            i = 1 - self.way(n)
            j = self.slot(2 * i - 1, n)
            recv(self.block(j), xs.at[self.k, n, 0], xr.at[self.k, n, i])
            return j

        def far(self, n):
            j = self.slot(2, n)
            recv(self.block(j), xs.at[self.k, n, 2], xr.at[self.k, n, 2])
            return j

    def w_slot(part, way, d):
        half = zh if part == 0 else 1 - zh
        yy = lax.rem(y + (8 - d if way == 0 else d), 8)
        return half * 8 + yy

    def ring_send(k, part, way, d):
        if d < REACH[part][way]:
            blk = wb.at[k, core, w_slot(part, way, d)]
            i = (part * 2 + way) * 4 + d
            send(blk, blk, rs.at[k, i], rr.at[k, i], y_up if way == 0 else y_down)

    def relay(k, j):
        blk = wb.at[k, core, j]
        send(blk, blk, bs.at[k, j], br.at[k, j], sibling)

    def on_ring(k, part, d, way):
        j = w_slot(part, way, d)
        i = (part * 2 + way) * 4 + d - 1
        recv(wb.at[k, core, j], rs.at[k, i], rr.at[k, i])
        ring_send(k, part, way, d)
        relay(k, j)

    def on_rings(k, part, d):
        for way in (0, 1):
            if d <= REACH[part][way]:
                on_ring(k, part, d, way)

    def to_half(k):
        own = wb.at[k, core, c]
        send(own, own, ps.at[k], pr.at[k], far_half)

    def own_ring(k):
        for way in (0, 1):
            ring_send(k, 0, way, 0)

    def on_half(k):
        j = (1 - zh) * 8 + y
        recv(wb.at[k, core, j], ps.at[k], pr.at[k])
        for way in (0, 1):
            ring_send(k, 1, way, 0)
        relay(k, j)

    halves = [TensorFlow(k, lambda j, k=k: xg.at[k, j]) for k in range(2)]
    own_ring(KV)
    to_half(KV)
    halves[0].own_z()
    halves[0].to_x(0)
    halves[1].own_z()
    halves[1].to_x(0)
    own_ring(Q)
    to_half(Q)
    relay(KV, c)
    relay(Q, c)

    pos_wide = jnp.transpose(jnp.broadcast_to(pos_ref[...].astype(F32), (HEAD_DIM, TOK)))
    angles = pos_wide * inv_ref[...]
    lane = lax.broadcasted_iota(jnp.int32, (TOK, HEAD_DIM), 1)
    trig[0] = jnp.cos(angles)
    sine = jnp.sin(angles)
    trig[1] = jnp.where(lane < HEAD_DIM // 2, -sine, sine)
    trig[2] = pos_wide

    sq[...] = jnp.zeros_like(sq)

    def take(k, j):
        block = xg[k, j].astype(F32)
        tokens = slice(k * 128, (k + 1) * 128)
        xt[j, 0, tokens] = jnp.transpose(block[0:HALF]).astype(BF16)
        xt[j, 1, tokens] = jnp.transpose(block[HALF:FEAT]).astype(BF16)
        sq[0:1, tokens] += jnp.sum(block * block, axis=0, keepdims=True)

    def on_z(n, k):
        halves[k].on_z(n)

    def relay_x(n, k):
        take(k, halves[k].relay_x(n))

    def near(n, k):
        take(k, halves[k].near(n))

    def far(n, k):
        take(k, halves[k].far(n))

    take(0, t)
    take(1, t)
    on_ring(KV, 0, 1, 0)
    on_ring(KV, 0, 1, 1)
    relay_x(0, 0)
    on_z(1, 0)
    near(0, 0)
    on_ring(Q, 0, 1, 0)
    on_ring(Q, 0, 1, 1)
    relay_x(0, 1)
    near(0, 1)
    far(0, 0)
    on_ring(KV, 0, 2, 0)
    on_ring(KV, 0, 2, 1)
    on_half(KV)
    take(0, halves[0].slot(0, 1))
    on_z(1, 1)
    relay_x(1, 0)
    on_ring(Q, 0, 2, 0)
    on_ring(Q, 0, 2, 1)
    on_z(2, 0)
    near(1, 0)
    far(0, 1)
    on_half(Q)
    take(1, halves[1].slot(0, 1))
    on_ring(KV, 0, 3, 0)
    on_ring(KV, 0, 3, 1)
    relay_x(1, 1)
    on_z(2, 1)
    send(wo_ref, wb.at[OUT, core, out_home], ms.at[0], mr.at[0], out_to, moves)

    @pl.when(jnp.logical_not(moves))
    def _():
        local = pltpu.make_async_copy(wo_ref, wb.at[OUT, core, c], loc)
        local.start()
        local.wait()
    take(0, halves[0].slot(0, 2))
    on_ring(KV, 1, 1, 0)
    on_ring(KV, 1, 1, 1)
    near(1, 1)
    far(1, 0)
    relay_x(2, 0)
    take(1, halves[1].slot(0, 2))
    on_z(3, 0)
    on_ring(Q, 0, 3, 0)
    on_ring(Q, 0, 3, 1)
    near(2, 0)
    far(1, 1)
    on_ring(Q, 1, 1, 0)
    on_ring(Q, 1, 1, 1)
    relay_x(2, 1)
    take(0, halves[0].slot(0, 3))
    on_z(3, 1)
    on_ring(KV, 0, 4, 0)
    on_ring(KV, 1, 2, 1)
    near(2, 1)
    far(2, 0)
    relay_x(3, 0)
    on_ring(KV, 1, 2, 0)
    on_ring(Q, 1, 2, 1)
    take(1, halves[1].slot(0, 3))
    near(3, 0)
    far(2, 1)
    on_ring(KV, 1, 3, 1)
    on_ring(Q, 0, 4, 0)
    relay_x(3, 1)
    on_ring(Q, 1, 2, 0)
    on_ring(Q, 1, 3, 1)
    recv(wb.at[OUT, core, c], ms.at[0], mr.at[0], moves)
    to_half(OUT)
    relay(OUT, c)
    near(3, 1)
    far(3, 0)
    on_ring(KV, 1, 3, 0)
    on_ring(KV, 1, 4, 1)
    far(3, 1)

    mean_sq = jnp.transpose(jnp.broadcast_to(sq[0:1, :], (HEAD_DIM, TOK))) / D

    def project(k):
        acc[...] = jnp.zeros_like(acc)

        def step(j, carry):
            recv(wb.at[k, other, j], bs.at[k, j], br.at[k, j])
            acc[...] += jnp.dot(xt[j, 0], wb[k, 0, j], preferred_element_type=F32) + jnp.dot(
                xt[j, 1], wb[k, 1, j], preferred_element_type=F32
            )
            return carry

        lax.fori_loop(0, 16, step, 0)

    def head(raw, gain_row):
        mean = jnp.mean(raw * raw, axis=-1, keepdims=True)
        unit = raw * lax.rsqrt(mean + EPS * (mean_sq + EPS)) * (1.0 + gain_row)
        return unit * trig[0] + pltpu.roll(unit, HEAD_DIM // 2, 1) * trig[1]

    project(KV)
    kv[4, 0] = head(acc[:, 0:128], kg_ref[...]).astype(BF16)
    kv[4, 1] = (acc[:, 128:256] * lax.rsqrt(mean_sq + EPS)).astype(BF16)

    for v in range(2):
        send(kv.at[4, v], kv.at[2, v], hs.at[0, v], hr.at[2, v], next_chip, c < 15)
        send(kv.at[4, v], kv.at[3, v], hs.at[2, v], hr.at[3, v], sibling, core == 0)
    for i in range(4):

        @pl.when(s + i < 4)
        def _():
            kv[i] = jnp.zeros((2, TOK, HEAD_DIM), BF16)

    on_ring(Q, 1, 3, 0)
    on_ring(Q, 1, 4, 1)
    project(Q)
    for i in range(2):
        qb[i] = head(acc[:, i * 128 : (i + 1) * 128], qg_ref[...]).astype(BF16)
    for v in range(2):
        recv(kv.at[2, v], hs.at[0, v], hr.at[2, v], c >= 1)
        send(kv.at[2, v], kv.at[0, v], hs.at[1, v], hr.at[0, v], next_chip, jnp.logical_and(c >= 1, c < 15))
        send(kv.at[2, v], kv.at[1 + 2 * core, v], hs.at[3, v], hr.at[1 + 2 * core, v], sibling, c >= 1)
    for v in range(2):
        recv(kv.at[0, v], hs.at[1, v], hr.at[0, v], c >= 2)
        send(kv.at[0, v], kv.at[1, v], hs.at[4, v], hr.at[1, v], sibling, jnp.logical_and(c >= 2, core == 1))
    own_ring(OUT)
    on_half(OUT)
    for v in range(2):
        recv(kv.at[3, v], hs.at[2, v], hr.at[3, v], s >= 1)
        recv(kv.at[1, v], hs.at[3, v], hr.at[1, v], s >= 3)

    ROWS = 128

    def attend(hd, r):
        rows = pl.ds(pl.multiple_of(r * ROWS, ROWS), ROWS)
        query = qb[hd, rows, :]
        position = trig[2, rows, :].astype(jnp.int32)
        position = jnp.concatenate([position, position], axis=1)
        row = lax.broadcasted_iota(jnp.int32, (ROWS, TOK), 0) + r * ROWS
        col = lax.broadcasted_iota(jnp.int32, (ROWS, TOK), 1)
        limit = jnp.minimum(jnp.minimum(position, row + s * TOK), WINDOW - 1)
        scores = []
        for i in range(5):
            raw = lax.dot_general(query, kv[i, 0], NT, preferred_element_type=F32)
            gap = row + (4 - i) * TOK - col
            allowed = gap <= limit
            if i == 4:
                allowed = jnp.logical_and(allowed, gap >= 0)
            scores.append(jnp.where(allowed, raw, -1e30))
        peak = scores[0]
        for i in range(1, 5):
            peak = jnp.maximum(peak, scores[i])
        peak = jnp.max(peak, axis=-1, keepdims=True)
        total = jnp.zeros((ROWS, TOK), F32)
        mixed = jnp.zeros((ROWS, HEAD_DIM), F32)
        for i in range(5):
            expo = jnp.exp2((scores[i] - peak) * (SCORE_SCALE * LOG2E))
            total += expo
            mixed += jnp.dot(expo.astype(BF16), kv[i, 1], preferred_element_type=F32)
        mixed = mixed / jnp.sum(total, axis=-1, keepdims=True)
        ctx[hd, t, rows, :] = mixed.astype(BF16)

    contexts = []
    for hd in range(2):

        def rows_of(r, carry, hd=hd):
            attend(hd, r)
            return carry

        lax.fori_loop(0, 2, rows_of, 0)
        flow = TensorFlow(2 + hd, lambda j, hd=hd: ctx.at[hd, j])
        flow.own_z()
        flow.to_x(0)
        contexts.append(flow)

    oacc[...] = jnp.zeros_like(oacc)

    def out_step(j):
        right = jnp.concatenate([ctx[0, j], ctx[1, j]], axis=1)
        place = lax.rem(j, 2) * 8 + lax.rem(t + j // 2, 8)
        for i in range(2):
            oacc[i] += lax.dot_general(wb[OUT, i, place], right, NT, preferred_element_type=F32)

    on_rings(OUT, 0, 1)
    on_rings(OUT, 1, 1)
    contexts[0].relay_x(0)
    contexts[0].on_z(1)
    contexts[1].relay_x(0)
    contexts[1].on_z(1)
    on_rings(OUT, 0, 2)
    on_rings(OUT, 1, 2)
    contexts[0].on_z(2)
    contexts[0].relay_x(1)
    contexts[1].on_z(2)
    contexts[1].relay_x(1)
    on_rings(OUT, 0, 3)
    on_rings(OUT, 1, 3)
    contexts[0].on_z(3)
    contexts[0].relay_x(2)
    contexts[1].on_z(3)
    contexts[1].relay_x(2)
    on_rings(OUT, 0, 4)
    on_rings(OUT, 1, 4)
    contexts[0].relay_x(3)
    contexts[1].relay_x(3)

    def drain():
        for copy, cond in pending:
            if cond is None:
                copy.wait_send()
            else:
                pl.when(cond)(copy.wait_send)
        pending.clear()

    drain()

    def wait_out(j, carry):
        recv(wb.at[OUT, other, j], bs.at[OUT, j], br.at[OUT, j])
        return carry

    lax.fori_loop(0, 16, wait_out, 0)
    out_step(t)
    for n in range(1, 4):
        out_step(contexts[0].slot(0, n))
    for n in range(4):
        out_step(contexts[0].slot(2 * contexts[0].way(n) - 1, n))
    for n in range(4):
        for flow in contexts:
            near = flow.near(n)
        out_step(near)
        for flow in contexts:
            far = flow.far(n)
        out_step(far)

    def spread(buf, k, me, device):
        for i, d in enumerate((1, 2, 3)):
            send(buf.at[me], buf.at[me], qs.at[k, i], qr.at[k, me], device(lax.rem(me + d, 4)))
        for d in (1, 2, 3):
            j = lax.rem(me + d, 4)
            recv(buf.at[j], qs.at[k, d - 1], qr.at[k, j])
        return buf[0] + buf[1] + buf[2] + buf[3]

    squares = jnp.sum(oacc[0] * oacc[0] + oacc[1] * oacc[1], axis=0, keepdims=True)
    zpart[zl] = jnp.broadcast_to(squares, (8, TOK))
    xpart[x] = spread(zpart, 0, zl, lambda j: at_tensor(x, j))
    squares = spread(xpart, 1, x, lambda j: at_tensor(j, zl))
    scale = lax.rsqrt(squares[0:1, :] / D + EPS)
    diagonal = lax.broadcasted_iota(jnp.int32, (FEAT, FEAT), 0) == lax.broadcasted_iota(
        jnp.int32, (FEAT, FEAT), 1
    )
    post_gain = 1.0 + jnp.sum(jnp.where(diagonal, pg_ref[...][None, :], 0.0), axis=1, keepdims=True)
    attention = jnp.concatenate([oacc[0], oacc[1]], axis=0)
    out_ref[...] = (h_ref[...].astype(F32) + attention * scale * post_gain).astype(BF16)

    drain()


def body(
    hidden_in,
    positions,
    pre_gain,
    query_weight,
    key_weight,
    value_weight,
    query_gain,
    key_gain,
    output_weight,
    post_gain,
):
    exponent = np.arange(HEAD_DIM // 2, dtype=np.float32) * np.float32(2.0) / np.float32(HEAD_DIM)
    inverse = np.float32(1.0) / np.float32(10000.0) ** exponent
    inverse = np.concatenate([inverse, inverse])[None, :].astype(np.float32)
    vmem = pl.BlockSpec(memory_space=pltpu.VMEM)
    dma = pltpu.SemaphoreType.DMA
    out = pl.pallas_call(
        kernel,
        out_shape=jax.ShapeDtypeStruct((FEAT, TOK), BF16),
        in_specs=[vmem] * 11,
        out_specs=vmem,
        scratch_shapes=[
            pltpu.VMEM((2, 16, FEAT, 128), BF16),
            pltpu.VMEM((16, 2, TOK, HALF), BF16),
            pltpu.VMEM((3, 2, 16, HALF, 256), BF16),
            pltpu.VMEM((5, 2, TOK, HEAD_DIM), BF16),
            pltpu.VMEM((2, TOK, HEAD_DIM), BF16),
            pltpu.VMEM((2, 16, TOK, HEAD_DIM), BF16),
            pltpu.VMEM((TOK, 256), F32),
            pltpu.VMEM((8, TOK), F32),
            pltpu.VMEM((3, TOK, HEAD_DIM), F32),
            pltpu.VMEM((2, HALF, TOK), F32),
            pltpu.VMEM((4, 8, TOK), F32),
            pltpu.VMEM((4, 8, TOK), F32),
            dma((4, 5)),
            dma((4, 4)),
            dma((4, 4, 3)),
            dma((4, 4, 3)),
            dma((3, 16)),
            dma((3, 16)),
            dma((3,)),
            dma((3,)),
            dma((3, 16)),
            dma((3, 16)),
            dma((1,)),
            dma((1,)),
            dma((5, 2)),
            dma((5, 2)),
            dma((2, 3)),
            dma((2, 4)),
            dma,
        ],
        compiler_params=pltpu.CompilerParams(
            collective_id=0, has_side_effects=True, vmem_limit_bytes=56 << 20
        ),
        cost_estimate=pl.CostEstimate(flops=3_000_000_000, bytes_accessed=1_000_000, transcendentals=1_000_000),
    )(
        hidden_in.T,
        positions[None, :],
        pre_gain.reshape(D // 128, 128),
        query_weight,
        key_weight,
        value_weight,
        query_gain[None, :],
        key_gain[None, :],
        output_weight.T,
        post_gain,
        inverse,
    )
    return out.T


def solution(mesh):
    placed = (
        P("seq", "tensor"),
        P("seq"),
        P(),
        P("seq", "tensor"),
        P("seq", "tensor"),
        P("seq", "tensor"),
        P(),
        P(),
        P("tensor", "seq"),
        P("tensor"),
    )
    return jax.shard_map(
        body, mesh=mesh, in_specs=placed, out_specs=P("seq", "tensor"), check_vma=False
    )
```

```python
import jax
import jax.numpy as jnp
import numpy as np
from jax import lax
from jax.experimental import pallas as pl
from jax.experimental.pallas import tpu as pltpu
from jax.sharding import PartitionSpec as P

D = 5376
HEAD_DIM = 128
WINDOW = 1024
FEAT = 336
HALF = 168
TOK = 256
EPS = 1e-6
SCORE_SCALE = 168.0**-0.5
LOG2E = 1.4426950408889634
MESH = pl.DeviceIdType.MESH
F32 = jnp.float32
BF16 = jnp.bfloat16

REACH = ((4, 3), (3, 4))
KV, Q, OUT = 0, 1, 2
NT = (((1,), (1,)), ((), ()))


def kernel(
    h_in,
    pos_ref,
    gain_ref,
    wq_in,
    wk_in,
    wv_in,
    qg_ref,
    kg_ref,
    wo_in,
    pg_ref,
    inv_ref,
    out_ref,
    h_ref,
    wq_ref,
    wk_ref,
    wv_ref,
    wo_ref,
    ld,
    xg,
    xt,
    wb,
    kv,
    qb,
    ctx,
    acc,
    sq,
    trig,
    oacc,
    zpart,
    xpart,
    zs,
    zr,
    xs,
    xr,
    rs,
    rr,
    ps,
    pr,
    bs,
    br,
    ms,
    mr,
    hs,
    hr,
    qs,
    qr,
    loc,
):
    s = lax.axis_index("seq")
    t = lax.axis_index("tensor")
    core = lax.rem(s, 2)
    c = s // 2
    y = lax.rem(c, 8)
    zh = c // 8
    x = t // 4
    zl = lax.rem(t, 4)
    other = 1 - core

    def at_seq(chip, which):
        return {"seq": chip * 2 + which, "tensor": t}

    def at_tensor(xx, zz):
        return {"seq": s, "tensor": lax.rem(xx + 8, 4) * 4 + zz}

    sibling = at_seq(c, other)
    far_half = at_seq((1 - zh) * 8 + y, core)
    y_up = at_seq(zh * 8 + lax.rem(y + 1, 8), core)
    y_down = at_seq(zh * 8 + lax.rem(y + 7, 8), core)
    next_chip = at_seq(lax.rem(c + 1, 16), core)
    prev_chip = at_seq(lax.rem(c + 15, 16), core)
    out_home = lax.rem(t, 2) * 8 + lax.rem(y + t // 2, 8)
    out_to = {"seq": out_home * 2 + core, "tensor": c}
    out_from = {"seq": t * 2 + core, "tensor": lax.rem(y + 8 - lax.rem(t, 8), 8) * 2 + zh}
    moves = jnp.logical_or(c != t, out_home != c)

    pending = []

    def send(src, dst, ssem, rsem, dev, cond=None):
        copy = pltpu.make_async_remote_copy(
            src_ref=src, dst_ref=dst, send_sem=ssem, recv_sem=rsem, device_id=dev, device_id_type=MESH
        )
        if cond is None:
            copy.start()
        else:
            pl.when(cond)(copy.start)
        pending.append((copy, cond))

    def recv(dst, ssem, rsem, cond=None):
        copy = pltpu.make_async_remote_copy(
            src_ref=dst, dst_ref=dst, send_sem=ssem, recv_sem=rsem, device_id=sibling, device_id_type=MESH
        )
        if cond is None:
            copy.wait_recv()
        else:
            pl.when(cond)(copy.wait_recv)

    barrier = pltpu.get_barrier_semaphore()
    peers = [sibling, far_half, y_up, y_down, next_chip, prev_chip]
    peers += [at_tensor(x + d, zl) for d in (1, 2, 3)]
    peers += [at_tensor(x, lax.rem(zl + d, 4)) for d in (1, 2, 3)]
    for peer in peers:
        pl.semaphore_signal(barrier, inc=1, device_id=peer, device_id_type=MESH)

    @pl.when(moves)
    def _():
        for peer in (out_to, out_from):
            pl.semaphore_signal(barrier, inc=1, device_id=peer, device_id_type=MESH)

    pairs = ((wk_in, wk_ref), (wv_in, wv_ref), (h_in, h_ref), (wq_in, wq_ref), (wo_in, wo_ref))
    loads = [pltpu.make_async_copy(src, dst, ld.at[i]) for i, (src, dst) in enumerate(pairs)]
    for copy in loads:
        copy.start()

    first = s * HALF
    row0 = first // 128
    index = lax.broadcasted_iota(jnp.int32, (HALF, 128), 0) + (first - row0 * 128)
    lanes = lax.broadcasted_iota(jnp.int32, (HALF, 128), 1)
    gain = jnp.zeros((HALF, 128), F32)
    for i in range(3):
        line = gain_ref[pl.ds(jnp.minimum(row0 + i, D // 128 - 1), 1), :]
        gain = jnp.where(lanes + i * 128 == index, line, gain)
    gain = 1.0 + jnp.sum(gain, axis=1, keepdims=True)
    for copy in loads:
        copy.wait()
    wb[KV, core, c, :, 0:128] = (wk_ref[...].astype(F32) * gain).astype(BF16)
    wb[KV, core, c, :, 128:256] = (wv_ref[...].astype(F32) * gain).astype(BF16)
    wb[Q, core, c] = (wq_ref[...].astype(F32) * gain).astype(BF16)

    xg[0, t] = h_ref[:, 0:128]
    xg[1, t] = h_ref[:, 128:256]
    pl.semaphore_wait(barrier, jnp.where(moves, len(peers) + 2, len(peers)))

    def near_z(n):
        if n == 0:
            return zl
        if n == 1:
            return zl + 1 - 2 * lax.rem(zl, 2)
        if n == 2:
            return 2 - zl // 2
        return 3 * (1 - zl // 2)

    class TensorFlow:
        def __init__(self, k, block):
            self.block = block
            self.k = k

        def slot(self, dx, n):
            return lax.rem(x + dx + 4, 4) * 4 + near_z(n)

        def way(self, n):
            return lax.rem(core + n, 2)

        def to_x(self, n):
            blk = self.block(self.slot(0, n))
            for i, d in enumerate((1, 3)):
                send(blk, blk, xs.at[self.k, n, i], xr.at[self.k, n, i], at_tensor(x + d, zl))

        def own_z(self):
            blk = self.block(t)
            send(blk, blk, zs.at[self.k, 0], zr.at[self.k, zl], at_tensor(x, lax.rem(zl + 1, 4)), zl < 3)
            send(blk, blk, zs.at[self.k, 4], zr.at[self.k, zl], at_tensor(x, lax.rem(zl + 3, 4)), zl > 0)

        def on_z(self, n):
            q = near_z(n)
            blk = self.block(self.slot(0, n))
            recv(blk, zs.at[self.k, n], zr.at[self.k, q])
            up = q < zl
            ok = jnp.where(up, zl < 3, zl > 0)
            dev = at_tensor(x, jnp.where(up, lax.rem(zl + 1, 4), lax.rem(zl + 3, 4)))
            send(blk, blk, zs.at[self.k, n], zr.at[self.k, q], dev, ok)
            self.to_x(n)

        def relay_x(self, n):
            i = self.way(n)
            d = 1 - 2 * i
            j = self.slot(-d, n)
            recv(self.block(j), xs.at[self.k, n, 0], xr.at[self.k, n, i])
            send(self.block(j), self.block(j), xs.at[self.k, n, 2], xr.at[self.k, n, 2], at_tensor(x + d, zl))
            return j

        def near(self, n):
            i = 1 - self.way(n)
            j = self.slot(2 * i - 1, n)
            recv(self.block(j), xs.at[self.k, n, 0], xr.at[self.k, n, i])
            return j

        def far(self, n):
            j = self.slot(2, n)
            recv(self.block(j), xs.at[self.k, n, 2], xr.at[self.k, n, 2])
            return j

    def w_slot(part, way, d):
        half = zh if part == 0 else 1 - zh
        yy = lax.rem(y + (8 - d if way == 0 else d), 8)
        return half * 8 + yy

    def ring_send(k, part, way, d):
        if d < REACH[part][way]:
            blk = wb.at[k, core, w_slot(part, way, d)]
            i = (part * 2 + way) * 4 + d
            send(blk, blk, rs.at[k, i], rr.at[k, i], y_up if way == 0 else y_down)

    def relay(k, j):
        blk = wb.at[k, core, j]
        send(blk, blk, bs.at[k, j], br.at[k, j], sibling)

    def on_ring(k, part, d, way):
        j = w_slot(part, way, d)
        i = (part * 2 + way) * 4 + d - 1
        recv(wb.at[k, core, j], rs.at[k, i], rr.at[k, i])
        ring_send(k, part, way, d)
        relay(k, j)

    def on_rings(k, part, d):
        for way in (0, 1):
            if d <= REACH[part][way]:
                on_ring(k, part, d, way)

    def to_half(k):
        own = wb.at[k, core, c]
        send(own, own, ps.at[k], pr.at[k], far_half)

    def own_ring(k):
        for way in (0, 1):
            ring_send(k, 0, way, 0)

    def on_half(k):
        j = (1 - zh) * 8 + y
        recv(wb.at[k, core, j], ps.at[k], pr.at[k])
        for way in (0, 1):
            ring_send(k, 1, way, 0)
        relay(k, j)

    halves = [TensorFlow(k, lambda j, k=k: xg.at[k, j]) for k in range(2)]
    own_ring(KV)
    to_half(KV)
    halves[0].own_z()
    halves[0].to_x(0)
    halves[1].own_z()
    halves[1].to_x(0)
    relay(KV, c)
    relay(Q, c)

    pos_wide = jnp.transpose(jnp.broadcast_to(pos_ref[...].astype(F32), (HEAD_DIM, TOK)))
    angles = pos_wide * inv_ref[...]
    lane = lax.broadcasted_iota(jnp.int32, (TOK, HEAD_DIM), 1)
    trig[0] = jnp.cos(angles)
    sine = jnp.sin(angles)
    trig[1] = jnp.where(lane < HEAD_DIM // 2, -sine, sine)
    trig[2] = pos_wide

    sq[...] = jnp.zeros_like(sq)

    def take(k, j):
        block = xg[k, j].astype(F32)
        tokens = slice(k * 128, (k + 1) * 128)
        xt[j, 0, tokens] = jnp.transpose(block[0:HALF]).astype(BF16)
        xt[j, 1, tokens] = jnp.transpose(block[HALF:FEAT]).astype(BF16)
        sq[0:1, tokens] += jnp.sum(block * block, axis=0, keepdims=True)

    def on_z(n, k):
        halves[k].on_z(n)

    def relay_x(n, k):
        take(k, halves[k].relay_x(n))

    def near(n, k):
        take(k, halves[k].near(n))

    def far(n, k):
        take(k, halves[k].far(n))

    take(0, t)
    take(1, t)
    on_ring(KV, 0, 1, 0)
    on_ring(KV, 0, 1, 1)
    relay_x(0, 0)
    own_ring(Q)
    to_half(Q)
    send(wo_ref, wb.at[OUT, core, out_home], ms.at[0], mr.at[0], out_to, moves)

    @pl.when(jnp.logical_not(moves))
    def _():
        local = pltpu.make_async_copy(wo_ref, wb.at[OUT, core, c], loc)
        local.start()
        local.wait()
    on_z(1, 0)
    near(0, 0)
    relay_x(0, 1)
    on_ring(KV, 0, 2, 0)
    on_ring(KV, 0, 2, 1)
    on_half(KV)
    near(0, 1)
    far(0, 0)
    take(0, halves[0].slot(0, 1))
    on_z(1, 1)
    relay_x(1, 0)
    on_ring(Q, 0, 1, 0)
    on_ring(Q, 0, 1, 1)
    on_z(2, 0)
    near(1, 0)
    far(0, 1)
    on_ring(KV, 0, 3, 0)
    on_ring(KV, 0, 3, 1)
    on_half(Q)
    take(1, halves[1].slot(0, 1))
    relay_x(1, 1)
    on_z(2, 1)
    on_ring(KV, 1, 1, 0)
    on_ring(KV, 1, 1, 1)
    take(0, halves[0].slot(0, 2))
    near(1, 1)
    far(1, 0)
    on_ring(Q, 0, 2, 0)
    on_ring(Q, 0, 2, 1)
    relay_x(2, 0)
    take(1, halves[1].slot(0, 2))
    on_z(3, 0)
    near(2, 0)
    far(1, 1)
    on_ring(KV, 0, 4, 0)
    on_ring(Q, 1, 1, 1)
    relay_x(2, 1)
    take(0, halves[0].slot(0, 3))
    on_z(3, 1)
    on_ring(KV, 1, 2, 1)
    on_ring(Q, 1, 1, 0)
    near(2, 1)
    far(2, 0)
    on_ring(KV, 1, 2, 0)
    on_ring(Q, 0, 3, 1)
    relay_x(3, 0)
    take(1, halves[1].slot(0, 3))
    recv(wb.at[OUT, core, c], ms.at[0], mr.at[0], moves)
    relay(OUT, c)
    to_half(OUT)
    near(3, 0)
    on_ring(Q, 0, 3, 0)
    on_ring(Q, 1, 2, 1)
    far(2, 1)
    relay_x(3, 1)
    on_ring(KV, 1, 3, 1)
    on_ring(Q, 1, 2, 0)
    near(3, 1)
    far(3, 0)
    on_ring(KV, 1, 3, 0)
    on_ring(Q, 1, 3, 1)
    far(3, 1)
    on_ring(KV, 1, 4, 1)
    on_ring(Q, 0, 4, 0)
    mean_sq = jnp.transpose(jnp.broadcast_to(sq[0:1, :], (HEAD_DIM, TOK))) / D

    def project(k):
        acc[...] = jnp.zeros_like(acc)

        def step(j, carry):
            recv(wb.at[k, other, j], bs.at[k, j], br.at[k, j])
            acc[...] += jnp.dot(xt[j, 0], wb[k, 0, j], preferred_element_type=F32) + jnp.dot(
                xt[j, 1], wb[k, 1, j], preferred_element_type=F32
            )
            return carry

        lax.fori_loop(0, 16, step, 0)

    def head(raw, gain_row):
        mean = jnp.mean(raw * raw, axis=-1, keepdims=True)
        unit = raw * lax.rsqrt(mean + EPS * (mean_sq + EPS)) * (1.0 + gain_row)
        return unit * trig[0] + pltpu.roll(unit, HEAD_DIM // 2, 1) * trig[1]

    project(KV)
    kv[4, 0] = head(acc[:, 0:128], kg_ref[...]).astype(BF16)
    kv[4, 1] = (acc[:, 128:256] * lax.rsqrt(mean_sq + EPS)).astype(BF16)

    for v in range(2):
        send(kv.at[4, v], kv.at[2, v], hs.at[0, v], hr.at[2, v], next_chip, c < 15)
        send(kv.at[4, v], kv.at[3, v], hs.at[2, v], hr.at[3, v], sibling, core == 0)
    for i in range(4):

        @pl.when(s + i < 4)
        def _():
            kv[i] = jnp.zeros((2, TOK, HEAD_DIM), BF16)

    on_ring(Q, 1, 3, 0)
    on_ring(Q, 1, 4, 1)
    project(Q)
    for i in range(2):
        qb[i] = head(acc[:, i * 128 : (i + 1) * 128], qg_ref[...]).astype(BF16)
    recv(kv.at[2, 0], hs.at[0, 0], hr.at[2, 0], c >= 1)
    send(kv.at[2, 0], kv.at[0, 0], hs.at[1, 0], hr.at[0, 0], next_chip, jnp.logical_and(c >= 1, c < 15))
    send(kv.at[2, 0], kv.at[1 + 2 * core, 0], hs.at[3, 0], hr.at[1 + 2 * core, 0], sibling, c >= 1)
    recv(kv.at[2, 1], hs.at[0, 1], hr.at[2, 1], c >= 1)
    send(kv.at[2, 1], kv.at[0, 1], hs.at[1, 1], hr.at[0, 1], next_chip, jnp.logical_and(c >= 1, c < 15))
    send(kv.at[2, 1], kv.at[1 + 2 * core, 1], hs.at[3, 1], hr.at[1 + 2 * core, 1], sibling, c >= 1)
    recv(kv.at[0, 0], hs.at[1, 0], hr.at[0, 0], c >= 2)
    send(kv.at[0, 0], kv.at[1, 0], hs.at[4, 0], hr.at[1, 0], sibling, jnp.logical_and(c >= 2, core == 1))
    recv(kv.at[0, 1], hs.at[1, 1], hr.at[0, 1], c >= 2)
    send(kv.at[0, 1], kv.at[1, 1], hs.at[4, 1], hr.at[1, 1], sibling, jnp.logical_and(c >= 2, core == 1))
    own_ring(OUT)
    on_half(OUT)
    for v in range(2):
        recv(kv.at[3, v], hs.at[2, v], hr.at[3, v], s >= 1)
        recv(kv.at[1, v], hs.at[3, v], hr.at[1, v], s >= 3)

    ROWS = 128

    def attend(hd, r):
        rows = pl.ds(pl.multiple_of(r * ROWS, ROWS), ROWS)
        query = qb[hd, rows, :]
        position = trig[2, rows, :].astype(jnp.int32)
        position = jnp.concatenate([position, position], axis=1)
        row = lax.broadcasted_iota(jnp.int32, (ROWS, TOK), 0) + r * ROWS
        col = lax.broadcasted_iota(jnp.int32, (ROWS, TOK), 1)
        limit = jnp.minimum(jnp.minimum(position, row + s * TOK), WINDOW - 1)
        scores = []
        for i in range(5):
            raw = lax.dot_general(query, kv[i, 0], NT, preferred_element_type=F32)
            gap = row + (4 - i) * TOK - col
            allowed = gap <= limit
            if i == 4:
                allowed = jnp.logical_and(allowed, gap >= 0)
            scores.append(jnp.where(allowed, raw, -1e30))
        peak = scores[0]
        for i in range(1, 5):
            peak = jnp.maximum(peak, scores[i])
        peak = jnp.max(peak, axis=-1, keepdims=True)
        total = jnp.zeros((ROWS, TOK), F32)
        mixed = jnp.zeros((ROWS, HEAD_DIM), F32)
        for i in range(5):
            expo = jnp.exp2((scores[i] - peak) * (SCORE_SCALE * LOG2E))
            total += expo
            mixed += jnp.dot(expo.astype(BF16), kv[i, 1], preferred_element_type=F32)
        mixed = mixed / jnp.sum(total, axis=-1, keepdims=True)
        ctx[hd, t, rows, :] = mixed.astype(BF16)

    contexts = []
    for hd in range(2):

        def rows_of(r, carry, hd=hd):
            attend(hd, r)
            return carry

        lax.fori_loop(0, 2, rows_of, 0)
        flow = TensorFlow(2 + hd, lambda j, hd=hd: ctx.at[hd, j])
        flow.own_z()
        flow.to_x(0)
        contexts.append(flow)

    oacc[...] = jnp.zeros_like(oacc)

    def out_step(j):
        right = jnp.concatenate([ctx[0, j], ctx[1, j]], axis=1)
        place = lax.rem(j, 2) * 8 + lax.rem(t + j // 2, 8)
        for i in range(2):
            oacc[i] += lax.dot_general(wb[OUT, i, place], right, NT, preferred_element_type=F32)

    on_rings(OUT, 0, 1)
    on_rings(OUT, 1, 1)
    contexts[0].relay_x(0)
    contexts[0].on_z(1)
    contexts[1].relay_x(0)
    contexts[1].on_z(1)
    on_rings(OUT, 0, 2)
    on_rings(OUT, 1, 2)
    contexts[0].on_z(2)
    contexts[0].relay_x(1)
    contexts[1].on_z(2)
    contexts[1].relay_x(1)
    on_rings(OUT, 0, 3)
    on_rings(OUT, 1, 3)
    contexts[0].on_z(3)
    contexts[0].relay_x(2)
    contexts[1].on_z(3)
    contexts[1].relay_x(2)
    on_rings(OUT, 0, 4)
    on_rings(OUT, 1, 4)
    contexts[0].relay_x(3)
    contexts[1].relay_x(3)

    def drain():
        for copy, cond in pending:
            if cond is None:
                copy.wait_send()
            else:
                pl.when(cond)(copy.wait_send)
        pending.clear()

    drain()

    def wait_out(j, carry):
        recv(wb.at[OUT, other, j], bs.at[OUT, j], br.at[OUT, j])
        return carry

    lax.fori_loop(0, 16, wait_out, 0)
    out_step(t)
    for n in range(1, 4):
        out_step(contexts[0].slot(0, n))
    for n in range(4):
        out_step(contexts[0].slot(2 * contexts[0].way(n) - 1, n))
    for n in range(4):
        for flow in contexts:
            near = flow.near(n)
        out_step(near)
        for flow in contexts:
            far = flow.far(n)
        out_step(far)

    def spread(buf, k, me, device):
        for i, d in enumerate((1, 2, 3)):
            send(buf.at[me], buf.at[me], qs.at[k, i], qr.at[k, me], device(lax.rem(me + d, 4)))
        for d in (1, 2, 3):
            j = lax.rem(me + d, 4)
            recv(buf.at[j], qs.at[k, d - 1], qr.at[k, j])
        return buf[0] + buf[1] + buf[2] + buf[3]

    squares = jnp.sum(oacc[0] * oacc[0] + oacc[1] * oacc[1], axis=0, keepdims=True)
    zpart[zl] = jnp.broadcast_to(squares, (8, TOK))
    xpart[x] = spread(zpart, 0, zl, lambda j: at_tensor(x, j))
    squares = spread(xpart, 1, x, lambda j: at_tensor(j, zl))
    scale = lax.rsqrt(squares[0:1, :] / D + EPS)
    diagonal = lax.broadcasted_iota(jnp.int32, (FEAT, FEAT), 0) == lax.broadcasted_iota(
        jnp.int32, (FEAT, FEAT), 1
    )
    post_gain = 1.0 + jnp.sum(jnp.where(diagonal, pg_ref[...][None, :], 0.0), axis=1, keepdims=True)
    attention = jnp.concatenate([oacc[0], oacc[1]], axis=0)
    out_ref[...] = (h_ref[...].astype(F32) + attention * scale * post_gain).astype(BF16)

    drain()


def body(
    hidden_in,
    positions,
    pre_gain,
    query_weight,
    key_weight,
    value_weight,
    query_gain,
    key_gain,
    output_weight,
    post_gain,
):
    exponent = np.arange(HEAD_DIM // 2, dtype=np.float32) * np.float32(2.0) / np.float32(HEAD_DIM)
    inverse = np.float32(1.0) / np.float32(10000.0) ** exponent
    inverse = np.concatenate([inverse, inverse])[None, :].astype(np.float32)
    vmem = pl.BlockSpec(memory_space=pltpu.VMEM)
    hbm = pl.BlockSpec(memory_space=pl.ANY)
    dma = pltpu.SemaphoreType.DMA
    out = pl.pallas_call(
        kernel,
        out_shape=jax.ShapeDtypeStruct((FEAT, TOK), BF16),
        in_specs=[hbm, vmem, vmem, hbm, hbm, hbm, vmem, vmem, hbm, vmem, vmem],
        out_specs=vmem,
        scratch_shapes=[
            pltpu.VMEM((FEAT, TOK), BF16),
            pltpu.VMEM((HALF, 256), BF16),
            pltpu.VMEM((HALF, 128), BF16),
            pltpu.VMEM((HALF, 128), BF16),
            pltpu.VMEM((HALF, 256), BF16),
            dma((5,)),
            pltpu.VMEM((2, 16, FEAT, 128), BF16),
            pltpu.VMEM((16, 2, TOK, HALF), BF16),
            pltpu.VMEM((3, 2, 16, HALF, 256), BF16),
            pltpu.VMEM((5, 2, TOK, HEAD_DIM), BF16),
            pltpu.VMEM((2, TOK, HEAD_DIM), BF16),
            pltpu.VMEM((2, 16, TOK, HEAD_DIM), BF16),
            pltpu.VMEM((TOK, 256), F32),
            pltpu.VMEM((8, TOK), F32),
            pltpu.VMEM((3, TOK, HEAD_DIM), F32),
            pltpu.VMEM((2, HALF, TOK), F32),
            pltpu.VMEM((4, 8, TOK), F32),
            pltpu.VMEM((4, 8, TOK), F32),
            dma((4, 5)),
            dma((4, 4)),
            dma((4, 4, 3)),
            dma((4, 4, 3)),
            dma((3, 16)),
            dma((3, 16)),
            dma((3,)),
            dma((3,)),
            dma((3, 16)),
            dma((3, 16)),
            dma((1,)),
            dma((1,)),
            dma((5, 2)),
            dma((5, 2)),
            dma((2, 3)),
            dma((2, 4)),
            dma,
        ],
        compiler_params=pltpu.CompilerParams(
            collective_id=0, has_side_effects=True, vmem_limit_bytes=56 << 20
        ),
        cost_estimate=pl.CostEstimate(flops=3_000_000_000, bytes_accessed=1_000_000, transcendentals=1_000_000),
    )(
        hidden_in.T,
        positions[None, :],
        pre_gain.reshape(D // 128, 128),
        query_weight,
        key_weight,
        value_weight,
        query_gain[None, :],
        key_gain[None, :],
        output_weight.T,
        post_gain,
        inverse,
    )
    return out.T


def solution(mesh):
    placed = (
        P("seq", "tensor"),
        P("seq"),
        P(),
        P("seq", "tensor"),
        P("seq", "tensor"),
        P("seq", "tensor"),
        P(),
        P(),
        P("tensor", "seq"),
        P("tensor"),
    )
    return jax.shard_map(
        body, mesh=mesh, in_specs=placed, out_specs=P("seq", "tensor"), check_vma=False
    )
```

```python
import jax
import jax.numpy as jnp
import numpy as np
from jax import lax
from jax.experimental import pallas as pl
from jax.experimental.pallas import tpu as pltpu
from jax.sharding import PartitionSpec as P

D = 5376
HEAD_DIM = 128
WINDOW = 1024
FEAT = 336
HALF = 168
TOK = 256
EPS = 1e-6
SCORE_SCALE = 168.0**-0.5
LOG2E = 1.4426950408889634
MESH = pl.DeviceIdType.MESH
F32 = jnp.float32
BF16 = jnp.bfloat16

REACH = ((4, 3), (3, 4))
KV, Q, OUT = 0, 1, 2
NT = (((1,), (1,)), ((), ()))


def kernel(
    h_in,
    pos_ref,
    gain_ref,
    wq_in,
    wk_in,
    wv_in,
    qg_ref,
    kg_ref,
    wo_in,
    pg_ref,
    inv_ref,
    out_ref,
    h_ref,
    wq_ref,
    wk_ref,
    wv_ref,
    wo_ref,
    ld,
    xg,
    xt,
    wb,
    kv,
    qb,
    ctx,
    acc,
    sq,
    trig,
    oacc,
    zpart,
    xpart,
    zs,
    zr,
    xs,
    xr,
    rs,
    rr,
    ps,
    pr,
    bs,
    br,
    ms,
    mr,
    hs,
    hr,
    qs,
    qr,
    loc,
    ws,
    wr,
):
    s = lax.axis_index("seq")
    t = lax.axis_index("tensor")
    core = lax.rem(s, 2)
    c = s // 2
    y = lax.rem(c, 8)
    zh = c // 8
    x = t // 4
    zl = lax.rem(t, 4)
    other = 1 - core

    def at_seq(chip, which):
        return {"seq": chip * 2 + which, "tensor": t}

    def at_tensor(xx, zz):
        return {"seq": s, "tensor": lax.rem(xx + 8, 4) * 4 + zz}

    sibling = at_seq(c, other)
    far_half = at_seq((1 - zh) * 8 + y, core)
    y_up = at_seq(zh * 8 + lax.rem(y + 1, 8), core)
    y_down = at_seq(zh * 8 + lax.rem(y + 7, 8), core)
    next_chip = at_seq(lax.rem(c + 1, 16), core)
    prev_chip = at_seq(lax.rem(c + 15, 16), core)
    out_home = lax.rem(t, 2) * 8 + lax.rem(y + t // 2, 8)
    out_to = {"seq": out_home * 2 + core, "tensor": c}
    out_from = {"seq": t * 2 + core, "tensor": lax.rem(y + 8 - lax.rem(t, 8), 8) * 2 + zh}
    moves = jnp.logical_or(c != t, out_home != c)

    pending = []

    def send(src, dst, ssem, rsem, dev, cond=None):
        copy = pltpu.make_async_remote_copy(
            src_ref=src, dst_ref=dst, send_sem=ssem, recv_sem=rsem, device_id=dev, device_id_type=MESH
        )
        if cond is None:
            copy.start()
        else:
            pl.when(cond)(copy.start)
        pending.append((copy, cond))

    def recv(dst, ssem, rsem, cond=None):
        copy = pltpu.make_async_remote_copy(
            src_ref=dst, dst_ref=dst, send_sem=ssem, recv_sem=rsem, device_id=sibling, device_id_type=MESH
        )
        if cond is None:
            copy.wait_recv()
        else:
            pl.when(cond)(copy.wait_recv)

    barrier = pltpu.get_barrier_semaphore()
    peers = [sibling, far_half, y_up, y_down, next_chip, prev_chip]
    peers += [at_tensor(x + d, zl) for d in (1, 2, 3)]
    peers += [at_tensor(x, lax.rem(zl + d, 4)) for d in (1, 2, 3)]
    for peer in peers:
        pl.semaphore_signal(barrier, inc=1, device_id=peer, device_id_type=MESH)

    @pl.when(moves)
    def _():
        for peer in (out_to, out_from):
            pl.semaphore_signal(barrier, inc=1, device_id=peer, device_id_type=MESH)

    pairs = ((wk_in, wk_ref), (wv_in, wv_ref), (h_in, h_ref), (wq_in, wq_ref), (wo_in, wo_ref))
    loads = [pltpu.make_async_copy(src, dst, ld.at[i]) for i, (src, dst) in enumerate(pairs)]
    for copy in loads:
        copy.start()

    first = s * HALF
    row0 = first // 128
    index = lax.broadcasted_iota(jnp.int32, (HALF, 128), 0) + (first - row0 * 128)
    lanes = lax.broadcasted_iota(jnp.int32, (HALF, 128), 1)
    gain = jnp.zeros((HALF, 128), F32)
    for i in range(3):
        line = gain_ref[pl.ds(jnp.minimum(row0 + i, D // 128 - 1), 1), :]
        gain = jnp.where(lanes + i * 128 == index, line, gain)
    gain = 1.0 + jnp.sum(gain, axis=1, keepdims=True)
    for copy in loads:
        copy.wait()
    wb[KV, core, c, :, 0:128] = (wk_ref[...].astype(F32) * gain).astype(BF16)
    wb[KV, core, c, :, 128:256] = (wv_ref[...].astype(F32) * gain).astype(BF16)
    wb[Q, core, c] = (wq_ref[...].astype(F32) * gain).astype(BF16)

    xg[0, t] = h_ref[:, 0:128]
    xg[1, t] = h_ref[:, 128:256]
    pl.semaphore_wait(barrier, jnp.where(moves, len(peers) + 2, len(peers)))

    def near_z(n):
        if n == 0:
            return zl
        if n == 1:
            return zl + 1 - 2 * lax.rem(zl, 2)
        if n == 2:
            return 2 - zl // 2
        return 3 * (1 - zl // 2)

    class TensorFlow:
        def __init__(self, k, block):
            self.block = block
            self.k = k

        def slot(self, dx, n):
            return lax.rem(x + dx + 4, 4) * 4 + near_z(n)

        def way(self, n):
            return lax.rem(core + n, 2)

        def to_x(self, n):
            blk = self.block(self.slot(0, n))
            for i, d in enumerate((1, 3)):
                send(blk, blk, xs.at[self.k, n, i], xr.at[self.k, n, i], at_tensor(x + d, zl))

        def own_z(self):
            blk = self.block(t)
            send(blk, blk, zs.at[self.k, 0], zr.at[self.k, zl], at_tensor(x, lax.rem(zl + 1, 4)), zl < 3)
            send(blk, blk, zs.at[self.k, 4], zr.at[self.k, zl], at_tensor(x, lax.rem(zl + 3, 4)), zl > 0)

        def on_z(self, n):
            q = near_z(n)
            blk = self.block(self.slot(0, n))
            recv(blk, zs.at[self.k, n], zr.at[self.k, q])
            up = q < zl
            ok = jnp.where(up, zl < 3, zl > 0)
            dev = at_tensor(x, jnp.where(up, lax.rem(zl + 1, 4), lax.rem(zl + 3, 4)))
            send(blk, blk, zs.at[self.k, n], zr.at[self.k, q], dev, ok)
            self.to_x(n)

        def relay_x(self, n):
            i = self.way(n)
            d = 1 - 2 * i
            j = self.slot(-d, n)
            recv(self.block(j), xs.at[self.k, n, 0], xr.at[self.k, n, i])
            send(self.block(j), self.block(j), xs.at[self.k, n, 2], xr.at[self.k, n, 2], at_tensor(x + d, zl))
            return j

        def near(self, n):
            i = 1 - self.way(n)
            j = self.slot(2 * i - 1, n)
            recv(self.block(j), xs.at[self.k, n, 0], xr.at[self.k, n, i])
            return j

        def far(self, n):
            j = self.slot(2, n)
            recv(self.block(j), xs.at[self.k, n, 2], xr.at[self.k, n, 2])
            return j

    class CrossFlow(TensorFlow):
        def step_x(self, near):
            d = 1 - 2 * self.way(0)
            if near:
                self.near(0)
                return lax.rem(4 + d, 4)
            self.relay_x(0)
            return lax.rem(4 - d, 4)

        def start_z(self, dx):
            blk = self.block(self.slot(dx, 0))
            send(blk, blk, ws.at[dx, 0], wr.at[dx, zl], at_tensor(x, lax.rem(zl + 1, 4)), zl < 3)
            send(blk, blk, ws.at[dx, 4], wr.at[dx, zl], at_tensor(x, lax.rem(zl + 3, 4)), zl > 0)

        def step_z(self, dx, n):
            q = near_z(n)
            blk = self.block(self.slot(dx, n))
            recv(blk, ws.at[dx, n], wr.at[dx, q])
            up = q < zl
            ok = jnp.where(up, zl < 3, zl > 0)
            dev = at_tensor(x, jnp.where(up, lax.rem(zl + 1, 4), lax.rem(zl + 3, 4)))
            send(blk, blk, ws.at[dx, n], wr.at[dx, q], dev, ok)

    def w_slot(part, way, d):
        half = zh if part == 0 else 1 - zh
        yy = lax.rem(y + (8 - d if way == 0 else d), 8)
        return half * 8 + yy

    def ring_send(k, part, way, d):
        if d < REACH[part][way]:
            blk = wb.at[k, core, w_slot(part, way, d)]
            i = (part * 2 + way) * 4 + d
            send(blk, blk, rs.at[k, i], rr.at[k, i], y_up if way == 0 else y_down)

    def relay(k, j):
        blk = wb.at[k, core, j]
        send(blk, blk, bs.at[k, j], br.at[k, j], sibling)

    def on_ring(k, part, d, way):
        j = w_slot(part, way, d)
        i = (part * 2 + way) * 4 + d - 1
        recv(wb.at[k, core, j], rs.at[k, i], rr.at[k, i])
        ring_send(k, part, way, d)
        relay(k, j)

    def on_rings(k, part, d):
        for way in (0, 1):
            if d <= REACH[part][way]:
                on_ring(k, part, d, way)

    def to_half(k):
        own = wb.at[k, core, c]
        send(own, own, ps.at[k], pr.at[k], far_half)

    def own_ring(k):
        for way in (0, 1):
            ring_send(k, 0, way, 0)

    def on_half(k):
        j = (1 - zh) * 8 + y
        recv(wb.at[k, core, j], ps.at[k], pr.at[k])
        for way in (0, 1):
            ring_send(k, 1, way, 0)
        relay(k, j)

    halves = [TensorFlow(k, lambda j, k=k: xg.at[k, j]) for k in range(2)]
    own_ring(KV)
    to_half(KV)
    halves[0].own_z()
    halves[0].to_x(0)
    halves[1].own_z()
    halves[1].to_x(0)
    relay(KV, c)
    relay(Q, c)

    pos_wide = jnp.transpose(jnp.broadcast_to(pos_ref[...].astype(F32), (HEAD_DIM, TOK)))
    angles = pos_wide * inv_ref[...]
    lane = lax.broadcasted_iota(jnp.int32, (TOK, HEAD_DIM), 1)
    trig[0] = jnp.cos(angles)
    sine = jnp.sin(angles)
    trig[1] = jnp.where(lane < HEAD_DIM // 2, -sine, sine)
    trig[2] = pos_wide

    sq[...] = jnp.zeros_like(sq)

    def take(k, j):
        block = xg[k, j].astype(F32)
        tokens = slice(k * 128, (k + 1) * 128)
        xt[j, 0, tokens] = jnp.transpose(block[0:HALF]).astype(BF16)
        xt[j, 1, tokens] = jnp.transpose(block[HALF:FEAT]).astype(BF16)
        sq[0:1, tokens] += jnp.sum(block * block, axis=0, keepdims=True)

    def on_z(n, k):
        halves[k].on_z(n)

    def relay_x(n, k):
        take(k, halves[k].relay_x(n))

    def near(n, k):
        take(k, halves[k].near(n))

    def far(n, k):
        take(k, halves[k].far(n))

    take(0, t)
    take(1, t)
    on_ring(KV, 0, 1, 0)
    on_ring(KV, 0, 1, 1)
    relay_x(0, 0)
    own_ring(Q)
    to_half(Q)
    send(wo_ref, wb.at[OUT, core, out_home], ms.at[0], mr.at[0], out_to, moves)

    @pl.when(jnp.logical_not(moves))
    def _():
        local = pltpu.make_async_copy(wo_ref, wb.at[OUT, core, c], loc)
        local.start()
        local.wait()
    on_z(1, 0)
    near(0, 0)
    relay_x(0, 1)
    on_ring(KV, 0, 2, 0)
    on_ring(KV, 0, 2, 1)
    on_half(KV)
    near(0, 1)
    far(0, 0)
    take(0, halves[0].slot(0, 1))
    on_z(1, 1)
    relay_x(1, 0)
    on_ring(Q, 0, 1, 0)
    on_ring(Q, 0, 1, 1)
    on_z(2, 0)
    near(1, 0)
    far(0, 1)
    on_ring(KV, 0, 3, 0)
    on_ring(KV, 0, 3, 1)
    on_half(Q)
    take(1, halves[1].slot(0, 1))
    relay_x(1, 1)
    on_z(2, 1)
    on_ring(KV, 1, 1, 0)
    on_ring(KV, 1, 1, 1)
    take(0, halves[0].slot(0, 2))
    near(1, 1)
    far(1, 0)
    on_ring(Q, 0, 2, 0)
    on_ring(Q, 0, 2, 1)
    relay_x(2, 0)
    take(1, halves[1].slot(0, 2))
    on_z(3, 0)
    near(2, 0)
    far(1, 1)
    on_ring(KV, 0, 4, 0)
    on_ring(Q, 1, 1, 1)
    relay_x(2, 1)
    take(0, halves[0].slot(0, 3))
    on_z(3, 1)
    on_ring(KV, 1, 2, 1)
    on_ring(Q, 1, 1, 0)
    near(2, 1)
    far(2, 0)
    on_ring(KV, 1, 2, 0)
    on_ring(Q, 0, 3, 1)
    relay_x(3, 0)
    take(1, halves[1].slot(0, 3))
    recv(wb.at[OUT, core, c], ms.at[0], mr.at[0], moves)
    relay(OUT, c)
    to_half(OUT)
    near(3, 0)
    on_ring(Q, 0, 3, 0)
    on_ring(Q, 1, 2, 1)
    far(2, 1)
    relay_x(3, 1)
    on_ring(KV, 1, 3, 1)
    on_ring(Q, 1, 2, 0)
    near(3, 1)
    far(3, 0)
    on_ring(KV, 1, 3, 0)
    on_ring(Q, 1, 3, 1)
    far(3, 1)
    on_ring(KV, 1, 4, 1)
    on_ring(Q, 0, 4, 0)
    mean_sq = jnp.transpose(jnp.broadcast_to(sq[0:1, :], (HEAD_DIM, TOK))) / D

    def project(k):
        acc[...] = jnp.zeros_like(acc)

        def step(j, carry):
            recv(wb.at[k, other, j], bs.at[k, j], br.at[k, j])
            acc[...] += jnp.dot(xt[j, 0], wb[k, 0, j], preferred_element_type=F32) + jnp.dot(
                xt[j, 1], wb[k, 1, j], preferred_element_type=F32
            )
            return carry

        lax.fori_loop(0, 16, step, 0)

    def head(raw, gain_row):
        mean = jnp.mean(raw * raw, axis=-1, keepdims=True)
        unit = raw * lax.rsqrt(mean + EPS * (mean_sq + EPS)) * (1.0 + gain_row)
        return unit * trig[0] + pltpu.roll(unit, HEAD_DIM // 2, 1) * trig[1]

    project(KV)
    kv[4, 0] = head(acc[:, 0:128], kg_ref[...]).astype(BF16)
    kv[4, 1] = (acc[:, 128:256] * lax.rsqrt(mean_sq + EPS)).astype(BF16)

    for v in range(2):
        send(kv.at[4, v], kv.at[2, v], hs.at[0, v], hr.at[2, v], next_chip, c < 15)
        send(kv.at[4, v], kv.at[3, v], hs.at[2, v], hr.at[3, v], sibling, core == 0)
    for i in range(4):

        @pl.when(s + i < 4)
        def _():
            kv[i] = jnp.zeros((2, TOK, HEAD_DIM), BF16)

    on_ring(Q, 1, 3, 0)
    on_ring(Q, 1, 4, 1)
    project(Q)
    for i in range(2):
        qb[i] = head(acc[:, i * 128 : (i + 1) * 128], qg_ref[...]).astype(BF16)
    recv(kv.at[2, 0], hs.at[0, 0], hr.at[2, 0], c >= 1)
    send(kv.at[2, 0], kv.at[0, 0], hs.at[1, 0], hr.at[0, 0], next_chip, jnp.logical_and(c >= 1, c < 15))
    send(kv.at[2, 0], kv.at[1 + 2 * core, 0], hs.at[3, 0], hr.at[1 + 2 * core, 0], sibling, c >= 1)
    recv(kv.at[2, 1], hs.at[0, 1], hr.at[2, 1], c >= 1)
    send(kv.at[2, 1], kv.at[0, 1], hs.at[1, 1], hr.at[0, 1], next_chip, jnp.logical_and(c >= 1, c < 15))
    send(kv.at[2, 1], kv.at[1 + 2 * core, 1], hs.at[3, 1], hr.at[1 + 2 * core, 1], sibling, c >= 1)
    recv(kv.at[0, 0], hs.at[1, 0], hr.at[0, 0], c >= 2)
    send(kv.at[0, 0], kv.at[1, 0], hs.at[4, 0], hr.at[1, 0], sibling, jnp.logical_and(c >= 2, core == 1))
    recv(kv.at[0, 1], hs.at[1, 1], hr.at[0, 1], c >= 2)
    send(kv.at[0, 1], kv.at[1, 1], hs.at[4, 1], hr.at[1, 1], sibling, jnp.logical_and(c >= 2, core == 1))
    own_ring(OUT)
    on_half(OUT)
    for v in range(2):
        recv(kv.at[3, v], hs.at[2, v], hr.at[3, v], s >= 1)
        recv(kv.at[1, v], hs.at[3, v], hr.at[1, v], s >= 3)

    ROWS = 128

    def attend(hd, r):
        rows = pl.ds(pl.multiple_of(r * ROWS, ROWS), ROWS)
        query = qb[hd, rows, :]
        position = trig[2, rows, :].astype(jnp.int32)
        position = jnp.concatenate([position, position], axis=1)
        row = lax.broadcasted_iota(jnp.int32, (ROWS, TOK), 0) + r * ROWS
        col = lax.broadcasted_iota(jnp.int32, (ROWS, TOK), 1)
        limit = jnp.minimum(jnp.minimum(position, row + s * TOK), WINDOW - 1)
        scores = []
        for i in range(5):
            raw = lax.dot_general(query, kv[i, 0], NT, preferred_element_type=F32)
            gap = row + (4 - i) * TOK - col
            allowed = gap <= limit
            if i == 4:
                allowed = jnp.logical_and(allowed, gap >= 0)
            scores.append(jnp.where(allowed, raw, -1e30))
        peak = scores[0]
        for i in range(1, 5):
            peak = jnp.maximum(peak, scores[i])
        peak = jnp.max(peak, axis=-1, keepdims=True)
        total = jnp.zeros((ROWS, TOK), F32)
        mixed = jnp.zeros((ROWS, HEAD_DIM), F32)
        for i in range(5):
            expo = jnp.exp2((scores[i] - peak) * (SCORE_SCALE * LOG2E))
            total += expo
            mixed += jnp.dot(expo.astype(BF16), kv[i, 1], preferred_element_type=F32)
        mixed = mixed / jnp.sum(total, axis=-1, keepdims=True)
        ctx[hd, t, rows, :] = mixed.astype(BF16)

    contexts = []
    for hd in range(2):

        def rows_of(r, carry, hd=hd):
            attend(hd, r)
            return carry

        lax.fori_loop(0, 2, rows_of, 0)
        if hd == 0:
            flow = TensorFlow(2, lambda j: ctx.at[0, j, pl.ds(128, 128)])
            cross = CrossFlow(4, lambda j: ctx.at[0, j, pl.ds(0, 128)])
        else:
            flow = TensorFlow(3, lambda j: ctx.at[1, j])
        flow.own_z()
        flow.to_x(0)
        if hd == 0:
            cross.to_x(0)
        contexts.append(flow)

    oacc[...] = jnp.zeros_like(oacc)

    def out_step(j):
        right = jnp.concatenate([ctx[0, j], ctx[1, j]], axis=1)
        place = lax.rem(j, 2) * 8 + lax.rem(t + j // 2, 8)
        for i in range(2):
            oacc[i] += lax.dot_general(wb[OUT, i, place], right, NT, preferred_element_type=F32)

    on_rings(OUT, 0, 1)
    on_rings(OUT, 1, 1)
    contexts[0].relay_x(0)
    contexts[0].on_z(1)
    dx_a = cross.step_x(False)
    dx_b = cross.step_x(True)
    contexts[1].relay_x(0)
    contexts[1].on_z(1)
    for dx in (0, dx_a, dx_b):
        cross.start_z(dx)
    on_rings(OUT, 0, 2)
    on_rings(OUT, 1, 2)
    contexts[0].on_z(2)
    cross.far(0)
    cross.start_z(2)
    contexts[0].relay_x(1)
    contexts[1].on_z(2)
    contexts[1].relay_x(1)
    for dx in (0, dx_a, dx_b):
        cross.step_z(dx, 1)
    on_rings(OUT, 0, 3)
    on_rings(OUT, 1, 3)
    contexts[0].on_z(3)
    contexts[0].relay_x(2)
    contexts[1].on_z(3)
    cross.step_z(2, 1)
    for dx in (0, dx_a):
        cross.step_z(dx, 2)
    contexts[1].relay_x(2)
    for dx in (dx_b, 2):
        cross.step_z(dx, 2)
    on_rings(OUT, 0, 4)
    on_rings(OUT, 1, 4)
    contexts[0].relay_x(3)
    contexts[1].relay_x(3)
    for dx in (0, dx_a, dx_b, 2):
        cross.step_z(dx, 3)

    def drain():
        for copy, cond in pending:
            if cond is None:
                copy.wait_send()
            else:
                pl.when(cond)(copy.wait_send)
        pending.clear()

    drain()

    def wait_out(j, carry):
        recv(wb.at[OUT, other, j], bs.at[OUT, j], br.at[OUT, j])
        return carry

    lax.fori_loop(0, 16, wait_out, 0)
    out_step(t)
    for n in range(1, 4):
        out_step(contexts[0].slot(0, n))
    for n in range(4):
        out_step(contexts[0].slot(2 * contexts[0].way(n) - 1, n))
    for n in range(4):
        for flow in contexts:
            near = flow.near(n)
        out_step(near)
        for flow in contexts:
            far = flow.far(n)
        out_step(far)

    def spread(buf, k, me, device):
        for i, d in enumerate((1, 2, 3)):
            send(buf.at[me], buf.at[me], qs.at[k, i], qr.at[k, me], device(lax.rem(me + d, 4)))
        for d in (1, 2, 3):
            j = lax.rem(me + d, 4)
            recv(buf.at[j], qs.at[k, d - 1], qr.at[k, j])
        return buf[0] + buf[1] + buf[2] + buf[3]

    squares = jnp.sum(oacc[0] * oacc[0] + oacc[1] * oacc[1], axis=0, keepdims=True)
    zpart[zl] = jnp.broadcast_to(squares, (8, TOK))
    xpart[x] = spread(zpart, 0, zl, lambda j: at_tensor(x, j))
    squares = spread(xpart, 1, x, lambda j: at_tensor(j, zl))
    scale = lax.rsqrt(squares[0:1, :] / D + EPS)
    diagonal = lax.broadcasted_iota(jnp.int32, (FEAT, FEAT), 0) == lax.broadcasted_iota(
        jnp.int32, (FEAT, FEAT), 1
    )
    post_gain = 1.0 + jnp.sum(jnp.where(diagonal, pg_ref[...][None, :], 0.0), axis=1, keepdims=True)
    attention = jnp.concatenate([oacc[0], oacc[1]], axis=0)
    out_ref[...] = (h_ref[...].astype(F32) + attention * scale * post_gain).astype(BF16)

    drain()


def body(
    hidden_in,
    positions,
    pre_gain,
    query_weight,
    key_weight,
    value_weight,
    query_gain,
    key_gain,
    output_weight,
    post_gain,
):
    exponent = np.arange(HEAD_DIM // 2, dtype=np.float32) * np.float32(2.0) / np.float32(HEAD_DIM)
    inverse = np.float32(1.0) / np.float32(10000.0) ** exponent
    inverse = np.concatenate([inverse, inverse])[None, :].astype(np.float32)
    vmem = pl.BlockSpec(memory_space=pltpu.VMEM)
    hbm = pl.BlockSpec(memory_space=pl.ANY)
    dma = pltpu.SemaphoreType.DMA
    out = pl.pallas_call(
        kernel,
        out_shape=jax.ShapeDtypeStruct((FEAT, TOK), BF16),
        in_specs=[hbm, vmem, vmem, hbm, hbm, hbm, vmem, vmem, hbm, vmem, vmem],
        out_specs=vmem,
        scratch_shapes=[
            pltpu.VMEM((FEAT, TOK), BF16),
            pltpu.VMEM((HALF, 256), BF16),
            pltpu.VMEM((HALF, 128), BF16),
            pltpu.VMEM((HALF, 128), BF16),
            pltpu.VMEM((HALF, 256), BF16),
            dma((5,)),
            pltpu.VMEM((2, 16, FEAT, 128), BF16),
            pltpu.VMEM((16, 2, TOK, HALF), BF16),
            pltpu.VMEM((3, 2, 16, HALF, 256), BF16),
            pltpu.VMEM((5, 2, TOK, HEAD_DIM), BF16),
            pltpu.VMEM((2, TOK, HEAD_DIM), BF16),
            pltpu.VMEM((2, 16, TOK, HEAD_DIM), BF16),
            pltpu.VMEM((TOK, 256), F32),
            pltpu.VMEM((8, TOK), F32),
            pltpu.VMEM((3, TOK, HEAD_DIM), F32),
            pltpu.VMEM((2, HALF, TOK), F32),
            pltpu.VMEM((4, 8, TOK), F32),
            pltpu.VMEM((4, 8, TOK), F32),
            dma((4, 5)),
            dma((4, 4)),
            dma((5, 4, 3)),
            dma((5, 4, 3)),
            dma((3, 16)),
            dma((3, 16)),
            dma((3,)),
            dma((3,)),
            dma((3, 16)),
            dma((3, 16)),
            dma((1,)),
            dma((1,)),
            dma((5, 2)),
            dma((5, 2)),
            dma((2, 3)),
            dma((2, 4)),
            dma,
            dma((4, 5)),
            dma((4, 4)),
        ],
        compiler_params=pltpu.CompilerParams(
            collective_id=0, has_side_effects=True, vmem_limit_bytes=56 << 20
        ),
        cost_estimate=pl.CostEstimate(flops=3_000_000_000, bytes_accessed=1_000_000, transcendentals=1_000_000),
    )(
        hidden_in.T,
        positions[None, :],
        pre_gain.reshape(D // 128, 128),
        query_weight,
        key_weight,
        value_weight,
        query_gain[None, :],
        key_gain[None, :],
        output_weight.T,
        post_gain,
        inverse,
    )
    return out.T


def solution(mesh):
    placed = (
        P("seq", "tensor"),
        P("seq"),
        P(),
        P("seq", "tensor"),
        P("seq", "tensor"),
        P("seq", "tensor"),
        P(),
        P(),
        P("tensor", "seq"),
        P("tensor"),
    )
    return jax.shard_map(
        body, mesh=mesh, in_specs=placed, out_specs=P("seq", "tensor"), check_vma=False
    )
```
